512 devices in a mesh: section: 2 (over core), grp: 128 (over y_lo, z, x), sub: 2 (over y_hi).
Axes of the slice: x: 4, y: 4 (y_hi: 2, y_lo: 2; y = y_hi * 2 + y_lo), z: 16, core: 2. Of those that a mesh axis runs over, the one named last changes fastest.
Arguments:
- phases: bfloat16 [600, 128, 8192], P(None, 'grp', ('section', 'sub')), may hold values from -8 to 8
- incidence: int32 [600, 2], replicated, may hold values from 0 to 255, as said below
- coherent: int32 [128, 8192], P('grp', ('section', 'sub')), may hold values 0 or 1
Outputs:
- corrected: bfloat16 [256, 128, 8192], P(None, 'grp', ('section', 'sub'))
- trend_fit: float32 [2, 128, 8192], P(None, 'grp', ('section', 'sub'))
The draws below stay inside these ranges and needn't reach their ends.
Inputs may be any that keep to these rules, and one draw needn't show every extreme that they name: `incidence`: row m holds the primary date and a later secondary date of interferogram m, 1 to 6 dates apart.
All inputs are finite; a program needn't handle non-finite values. No bound on the sum of `coherent` on one device may be relied on, other than what follows from the above.
Results may differ from the reference program's by a relative error of at most 0.0064.
Values may be sent and summed in bfloat16 or wider, within the bound.
A program may use at most 64 MiB of HBM per device.

```python
import math
import jax
import jax.numpy as jnp
from jax import lax

IFGS = 600
COLS = 8192
FREQS = 256
DATES = 256
ROWS = 128


def draw_incidence(key, part):
    key = jax.random.fold_in(key, 7)
    later_key, gap_key = jax.random.split(key)
    later = jax.random.randint(later_key, (IFGS,), 1, DATES)
    spacing = jax.random.randint(gap_key, (IFGS,), 1, 7)
    later = later.at[0].set(DATES - 1).at[1].set(spacing[1])
    earlier = jnp.maximum(later - spacing, 0)
    return jnp.stack([earlier, later], axis=1).astype(jnp.int32)


def draw_phases(key, part):
    key = jax.random.fold_in(key, 13)
    row_ids = jnp.arange(ROWS, dtype=jnp.int32)[:, None]
    col_ids = jnp.arange(COLS, dtype=jnp.int32)[None, :]

    def one_ifg(number):
        ifg_key = jax.random.fold_in(key, number)
        sub_keys = jax.random.split(ifg_key, 7)
        speckle = jnp.clip(jax.random.normal(sub_keys[1], (ROWS, COLS), jnp.float32), -4.0, 4.0)
        amplitude = 1.0
        wave_rows = jax.random.randint(sub_keys[3], (3,), 0, 6)
        wave_cols = jax.random.randint(sub_keys[4], (3,), 1, 48)
        shifts = jax.random.uniform(sub_keys[5], (3,), jnp.float32, -math.pi, math.pi)
        heights = jax.random.uniform(sub_keys[6], (3,), jnp.float32, -amplitude, amplitude)
        phase_field = speckle
        for wave_index in range(3):
            row_turns = (wave_rows[wave_index] * row_ids % ROWS).astype(jnp.float32) / ROWS
            col_turns = (wave_cols[wave_index] * col_ids % COLS).astype(jnp.float32) / COLS
            phase_field = phase_field + heights[wave_index] * jnp.sin(2.0 * math.pi * (row_turns + col_turns) + shifts[wave_index])
        return phase_field.astype(jnp.bfloat16)
    return lax.map(one_ifg, jnp.arange(IFGS, dtype=jnp.int32))


def plant(entries, rng, low, high):
    dims = entries.shape
    spot = [jax.random.randint(jax.random.fold_in(rng, axis), (), 0, dims[axis]) for axis in range(len(dims))]
    entries = entries.at[tuple(spot)].set(low)
    longest = dims.index(max(dims))
    spot[longest] = (spot[longest] + 1) % dims[longest]
    return entries.at[tuple(spot)].set(high)


def setup_inputs(seed: int = 0) -> dict:
    key_list = jax.random.split(jax.random.key(seed), 4)
    return {
        "phases": draw_phases(jax.random.fold_in(key_list[3], 71), 0),
        "incidence": draw_incidence(jax.random.fold_in(key_list[3], 71), 0),
        "coherent": plant((jax.random.randint(key_list[2], (ROWS, COLS), 0, 8) < 7).astype(jnp.int32), jax.random.fold_in(key_list[2], 1), 0, 1),
    }


REG = 0.1

def column_table(first_col, col_count, freq_count, col_total):
    frequency = jnp.arange(freq_count, dtype=jnp.int32)[:, None]
    column = first_col + jnp.arange(col_count, dtype=jnp.int32)[None, :]
    phase_turns = (frequency * column % col_total).astype(jnp.float32) * (2.0 * math.pi / col_total)
    return jnp.concatenate([jnp.cos(phase_turns), -jnp.sin(phase_turns)], axis=0).astype(jnp.bfloat16)

def row_filter(row_total):
    indices = jnp.arange(row_total, dtype=jnp.int32)
    frequency = jnp.minimum(indices, row_total - indices).astype(jnp.float32)
    taper = jnp.exp(-jnp.square(frequency / (row_total / 4.0)))
    phase_turns = (indices[:, None] * indices[None, :] % row_total).astype(jnp.float32) * (2.0 * math.pi / row_total)
    cos_rows = jnp.cos(phase_turns)
    sin_rows = jnp.sin(phase_turns)
    first_part = jnp.dot((cos_rows * taper[None, :]).astype(jnp.float32), cos_rows.T.astype(jnp.float32), precision=lax.Precision.HIGHEST, preferred_element_type=jnp.float32)
    second_part = jnp.dot((sin_rows * taper[None, :]).astype(jnp.float32), sin_rows.T.astype(jnp.float32), precision=lax.Precision.HIGHEST, preferred_element_type=jnp.float32)
    return (first_part + second_part) / row_total

def column_scale(freq_count, col_total):
    frequency = jnp.arange(freq_count, dtype=jnp.int32).astype(jnp.float32)
    doubling = jnp.where(frequency == 0.0, 1.0, 2.0)
    col_scale = doubling * jnp.exp(-jnp.square(frequency / freq_count)) / col_total
    return jnp.concatenate([col_scale, col_scale])

def pseudo_inverse(incidence, date_total):
    date_ids = jnp.arange(date_total, dtype=jnp.int32)[None, :]
    design = (incidence[:, 1:2] == date_ids).astype(jnp.float32) - (incidence[:, 0:1] == date_ids).astype(jnp.float32)
    normal = jnp.dot(design.T.astype(jnp.float32), design.astype(jnp.float32), precision=lax.Precision.HIGHEST, preferred_element_type=jnp.float32)
    normal = normal + REG * jnp.eye(date_total, dtype=jnp.float32)
    factor = jnp.linalg.cholesky(normal)
    return jax.scipy.linalg.cho_solve((factor, True), design.T).astype(jnp.bfloat16)

def detrend(series, live_pixels):
    date_count = series.shape[0]
    epochs = (2.0 * jnp.arange(date_count, dtype=jnp.float32) - (date_count - 1)) / (date_count - 1)
    offset = jnp.sum(series, axis=0) / date_count
    velocity = jnp.sum(epochs[:, None] * series, axis=0) / jnp.sum(epochs * epochs)
    residual = live_pixels[None, :] * (series - offset[None, :] - epochs[:, None] * velocity[None, :])
    return (offset, velocity, residual.astype(jnp.bfloat16))

def reference(phases, incidence, coherent):
    inverse_map = pseudo_inverse(incidence, DATES)
    flat_phases = phases.reshape(IFGS, ROWS * COLS)
    series = jnp.dot(inverse_map.astype(jnp.float32), flat_phases.astype(jnp.float32), preferred_element_type=jnp.float32)
    live_pixels = coherent.reshape(ROWS * COLS).astype(jnp.float32)
    offset, velocity, residual = detrend(series, live_pixels)
    col_table = column_table(0, COLS, FREQS, COLS)
    row_smoother = row_filter(ROWS)
    col_scale = column_scale(FREQS, COLS)

    def smooth_date(date_image):
        spectrum = jnp.dot(date_image.astype(jnp.float32), col_table.T.astype(jnp.float32), preferred_element_type=jnp.float32)
        smoothed = jnp.dot(row_smoother.astype(jnp.float32), spectrum.astype(jnp.float32), precision=lax.Precision.HIGHEST, preferred_element_type=jnp.float32)
        weights = (smoothed * col_scale[None, :]).astype(jnp.bfloat16)
        return jnp.dot(weights.astype(jnp.float32), col_table.astype(jnp.float32), preferred_element_type=jnp.float32).astype(jnp.bfloat16)
    screen = lax.map(smooth_date, residual.reshape(DATES, ROWS, COLS))
    screen_flat = screen.reshape(DATES, ROWS * COLS).astype(jnp.float32)
    corrected = (live_pixels[None, :] * (series - screen_flat)).astype(jnp.bfloat16)
    trend_fit = jnp.stack([offset, velocity]).reshape(2, ROWS, COLS)
    return (corrected.reshape(DATES, ROWS, COLS), trend_fit)
```

```python
import functools
import math

import jax
import jax.numpy as jnp
import numpy as np
from jax import lax
from jax.experimental import pallas as pl
from jax.experimental.pallas import tpu as pltpu
from jax.sharding import PartitionSpec as P

MESH = pl.DeviceIdType.MESH
HIGHEST = lax.Precision.HIGHEST
F32 = jnp.float32
BF16 = jnp.bfloat16

REG = 0.1
FREQS = 256
DATES = 256
ROWS = 128
COLS = 8192
BLOCKS = DATES // 8
COL_DEV = 2048
TILE = 512

PLANE = 32
DEPTH = 16
SHELF = 8


def angle_tables():
    frequency = np.arange(FREQS, dtype=np.int64)[:, None]
    column = np.arange(128, dtype=np.int64)[None, :]
    start = (frequency * column % COLS) * (2.0 * math.pi / COLS)
    step = (frequency * np.full_like(column, 128) % COLS) * (2.0 * math.pi / COLS)
    return np.stack([np.cos(start), np.sin(start), np.cos(step), np.sin(step)]).astype(np.float32)


def row_filter():
    indices = np.arange(ROWS)
    frequency = np.minimum(indices, ROWS - indices).astype(np.float64)
    taper = np.exp(-np.square(frequency / (ROWS / 4.0)))
    turns = (indices[:, None] * indices[None, :] % ROWS) * (2.0 * math.pi / ROWS)
    cos_rows, sin_rows = np.cos(turns), np.sin(turns)
    return ((cos_rows * taper) @ cos_rows.T + (sin_rows * taper) @ sin_rows.T) / ROWS


def smoothing_matrix():
    index = np.arange(DEPTH * SHELF * 2)
    z, shelf, half = index // 16, index // 2 % 8, index % 2
    row = shelf // 4 * 64 + z * 4 + shelf % 4
    full = row_filter()[row[:, None], row[None, :]] * (half[:, None] == half[None, :])
    return full.astype(np.float32)


def column_scales():
    frequency = np.arange(FREQS)
    scale = np.where(frequency == 0, 1.0, 2.0) * np.exp(-np.square(frequency / FREQS)) / COLS
    return scale.astype(np.float32).reshape(2, 1, 128)


def iota(shape, axis):
    return lax.broadcasted_iota(jnp.int32, shape, axis)


def hot(condition):
    return jnp.where(condition, 1.0, 0.0).astype(F32)


def dot(a, b, precision=None):
    return jnp.dot(a, b, precision=precision, preferred_element_type=F32)


def dot_nt(a, b, precision=None):
    return lax.dot_general(
        a, b, (((1,), (1,)), ((), ())), precision=precision, preferred_element_type=F32
    )


def lane_roll(x, shift):
    flat = x.reshape(64, 128)
    return pltpu.roll(flat, shift, 1).reshape(8, 8, 128)


def block_product(a, b):
    total = a[:, 0:1, :] * b[0][None]
    for k in range(1, 8):
        total = total + a[:, k : k + 1, :] * b[k][None]
    return total


def block_inverse(d):
    sub = iota((8, 128), 0)
    rows = [d[i] for i in range(8)]
    for k in range(8):
        pivot = 1.0 / rows[k][k : k + 1, :]
        pivot_row = jnp.where(sub == k, pivot, rows[k] * pivot)
        for i in range(8):
            if i != k:
                factor = rows[i][k : k + 1, :]
                rows[i] = jnp.where(sub == k, 0.0, rows[i]) - factor * pivot_row
        rows[k] = pivot_row
    return jnp.stack(rows)


def pseudo_inverse(incidence):
    count = incidence.shape[1]
    primary, secondary = incidence[0:1, :], incidence[1:2, :]
    dates = iota((DATES, count), 0)
    design_t = hot(dates == secondary) - hot(dates == primary)
    p_in, p_block, s_in, s_block = primary & 7, primary >> 3, secondary & 7, secondary >> 3
    block = iota((128, count), 0) & (BLOCKS - 1)
    at_primary = hot(block == p_block).astype(BF16)
    at_secondary = hot(block == s_block).astype(BF16)
    pair = iota((64, count), 0)
    same = hot(p_block == s_block)
    ps = hot(pair == p_in * 8 + s_in)
    sp = hot(pair == s_in * 8 + p_in)
    on_primary = hot(pair == p_in * 9) - same * (ps + sp)
    on_secondary = hot(pair == s_in * 9)
    to_next = (same - 1.0) * ps
    to_last = (same - 1.0) * sp
    from_primary = dot_nt(jnp.concatenate([on_primary, to_next], 0).astype(BF16), at_primary)
    from_secondary = dot_nt(jnp.concatenate([on_secondary, to_last], 0).astype(BF16), at_secondary)
    entry = iota((64, 128), 0)
    eye = hot((entry >> 3) == (entry & 7))
    diag = (from_primary[:64] + from_secondary[:64] + REG * eye).reshape(8, 8, 128)
    below = from_secondary[64:].reshape(8, 8, 128)
    above = from_primary[64:].reshape(8, 8, 128)
    first = (iota((8, 8, 128), 2) & BLOCKS) == 0

    date = iota((DATES, 128), 0)
    lane = iota((DATES, 128), 1)
    take_first = hot((date >> 3) == lane)
    take_second = hot((date >> 3) == lane - BLOCKS)
    own_row = (iota((DATES, 64), 1) >> 3) == (iota((DATES, 64), 0) & 7)
    spread = hot((iota((64, DATES), 1) & 7) == (iota((64, DATES), 0) & 7))
    row_block = iota((DATES, DATES), 0) >> 3
    col_block = iota((DATES, DATES), 1) >> 3

    def dense(take, x, shift):
        rows = jnp.where(own_row, dot_nt(take, x.reshape(64, 128), HIGHEST), 0.0)
        return jnp.where(col_block == row_block + shift, dot(rows, spread, HIGHEST), 0.0)

    total = None
    step = 1
    while step < BLOCKS:
        inverse = block_inverse(diag)
        near = jnp.where(first, lane_roll(inverse, step), lane_roll(inverse, 128 - step))
        gain = block_product(jnp.where(first, below, above), near)
        back = jnp.where(first, lane_roll(above, step), lane_roll(below, 128 - step))
        change = block_product(gain, back)
        diag = diag - change - lane_roll(change, BLOCKS)
        gamma = dense(take_first, gain, -step) + dense(take_second, gain, step)
        if total is None:
            total = hot(iota((DATES, DATES), 0) == iota((DATES, DATES), 1)) - gamma
        else:
            total = total - dot(gamma, total, HIGHEST)
        if 2 * step < BLOCKS:
            far = jnp.where(first, lane_roll(below, step), lane_roll(above, 128 - step))
            links = -block_product(gain, far)
            swapped = lane_roll(links, BLOCKS)
            below = jnp.where(first, links, swapped)
            above = jnp.where(first, swapped, links)
        step *= 2
    final = dense(take_first, block_inverse(diag), 0)
    return dot(dot(final, total, HIGHEST), design_t, HIGHEST).astype(BF16)


def part_index():
    return lax.axis_index("section") * 2 + lax.axis_index("sub")


def fill_table(angles_ref, table_ref):
    @pl.loop(0, FREQS // 16)
    def _(group):
        first = pl.multiple_of(group * 16, 16)
        rows, sin_rows = pl.ds(first, 16), pl.ds(first + FREQS, 16)
        cos, sin = angles_ref[0, rows, :], angles_ref[1, rows, :]
        step_cos, step_sin = angles_ref[2, rows, :], angles_ref[3, rows, :]
        quarter = ((iota((16, 128), 0) + first) * part_index()) & 3
        odd, minus = (quarter & 1) == 1, quarter >= 2
        cos, sin = jnp.where(odd, -sin, cos), jnp.where(odd, cos, sin)
        cos, sin = jnp.where(minus, -cos, cos), jnp.where(minus, -sin, sin)
        for tile in range(COL_DEV // 128):
            cols = slice(tile * 128, tile * 128 + 128)
            table_ref[rows, cols] = cos.astype(BF16)
            table_ref[sin_rows, cols] = (-sin).astype(BF16)
            cos, sin = cos * step_cos - sin * step_sin, sin * step_cos + cos * step_sin


def regroup_matrix(inverse):
    out, source = iota((256, 256), 0), iota((256, 256), 1)
    if inverse:
        out, source = source, out
    return hot(source == ((out >> 1) & 7) * 32 + (out >> 4) * 2 + (out & 1)).astype(BF16)


def series_kernel(
    incidence_ref,
    coherent_ref,
    angles_ref,
    phases_hbm,
    series_ref,
    trend_ref,
    spectrum_ref,
    table_ref,
    phases_ref,
    map_ref,
    total_ref,
    sem,
):
    load_phases = pltpu.make_async_copy(phases_hbm, phases_ref, sem)
    load_phases.start()
    fill_table(angles_ref, table_ref)
    map_ref[...] = pseudo_inverse(incidence_ref[...])
    total_ref[...] = jnp.zeros_like(total_ref)
    load_phases.wait()
    epochs = (2.0 * iota((DATES, 1), 0).astype(F32) - (DATES - 1)) / (DATES - 1)
    spread = sum(((2.0 * n - (DATES - 1)) / (DATES - 1)) ** 2 for n in range(DATES))

    @pl.loop(0, COL_DEV // TILE)
    def _(tile):
        cols = pl.ds(pl.multiple_of(tile * TILE, TILE), TILE)
        series = dot(map_ref[...], phases_ref[:, cols])
        series_ref[:, cols] = series
        offset = jnp.sum(series, axis=0, keepdims=True) / DATES
        rate = jnp.sum(epochs * series, axis=0, keepdims=True) / spread
        trend_ref[0, :, cols] = offset
        trend_ref[1, :, cols] = rate
        live = coherent_ref[:, cols].astype(F32)
        residual = (live * (series - offset - epochs * rate)).astype(BF16)
        total_ref[...] += dot_nt(residual, table_ref[:, cols])

    for nb in range(8):
        for jb in range(4):
            spectrum_ref[nb * 4 + jb] = total_ref[
                nb * 32 : nb * 32 + 32, jb * 128 : jb * 128 + 128
            ].astype(BF16)


def exchange_kernel(
    spectrum_ref,
    smooth_ref,
    scale_ref,
    weights_ref,
    part_in,
    up_out,
    up_in,
    down_out,
    down_in,
    part_out,
    back_in,
    send_a,
    recv_a,
    send_b,
    recv_b,
    send_c,
    recv_c,
    send_d,
    recv_d,
):
    section, grp, sub = (lax.axis_index(name) for name in ("section", "grp", "sub"))
    shelf = grp // 64 * 4 + grp % 4
    z = grp // 4 % 16
    me = (section * 2 + sub) * 8 + shelf

    def in_plane(other):
        return (
            other // 16,
            other // 4 % 2 * 64 + z * 4 + other % 4,
            other // 8 % 2,
        )

    def along_z(other):
        return (section, grp // 64 * 64 + other * 4 + grp % 4, sub)

    barrier = pltpu.get_barrier_semaphore()

    @pl.loop(1, PLANE)
    def _(hop):
        pl.semaphore_signal(
            barrier, inc=1, device_id=in_plane((me + hop) % PLANE), device_id_type=MESH
        )

    @pl.loop(1, DEPTH)
    def _(hop):
        pl.semaphore_signal(
            barrier, inc=1, device_id=along_z((z + hop) % DEPTH), device_id_type=MESH
        )

    pl.semaphore_wait(barrier, PLANE - 1 + DEPTH - 1)

    def gather(size, mine, source, target, send, recv, where):
        def copy(other, slot, held):
            return pltpu.make_async_remote_copy(
                src_ref=source(other),
                dst_ref=target.at[slot],
                send_sem=send.at[held],
                recv_sem=recv.at[slot],
                device_id=where(other),
                device_id_type=MESH,
            )

        @pl.loop(1, size)
        def _(hop):
            other = (mine + hop) % size
            copy(other, mine, other).start()

        target[mine] = source(mine)[...]

        @pl.loop(1, size)
        def _(hop):
            other = (mine + hop) % size
            copy(other, other, other).wait_recv()

        def finish():
            @pl.loop(1, size)
            def _(hop):
                other = (mine + hop) % size
                copy(other, mine, other).wait_send()

        return finish

    done_a = gather(
        PLANE, me, lambda o: spectrum_ref.at[o], part_in, send_a, recv_a, in_plane
    )
    row_sum = jnp.sum(part_in[...].astype(F32).reshape(4, 256, 128), axis=0).astype(BF16)
    up_out[...] = dot(regroup_matrix(False), row_sum).astype(BF16).reshape(DEPTH, 16, 128)
    done_b = gather(DEPTH, z, lambda o: up_out.at[o], up_in, send_b, recv_b, along_z)
    rows = up_in[...].reshape(256, 128)
    smooth = smooth_ref[...]
    smooth_high = smooth.astype(BF16)
    smooth_low = (smooth - smooth_high.astype(F32)).astype(BF16)
    smoothed = dot(smooth_high, rows) + dot(smooth_low, rows)
    weights = (smoothed * scale_ref[me % 2]).astype(BF16)
    down_out[...] = weights.reshape(DEPTH, 16, 128)
    done_c = gather(DEPTH, z, lambda o: down_out.at[o], down_in, send_c, recv_c, along_z)
    whole = down_in[...].reshape(256, 128)
    part_out[...] = dot(regroup_matrix(True), whole).astype(BF16).reshape(SHELF, 32, 128)
    done_d = gather(
        PLANE, me, lambda o: part_out.at[o % SHELF], back_in, send_d, recv_d, in_plane
    )
    weights_ref[...] = back_in[...]
    done_a()
    done_b()
    done_c()
    done_d()


def correct_kernel(
    coherent_ref, series_ref, weights_ref, table_ref, corrected_ref, flat_ref
):
    for nb in range(8):
        for jb in range(4):
            flat_ref[nb * 32 : nb * 32 + 32, jb * 128 : jb * 128 + 128] = weights_ref[nb * 4 + jb]

    @pl.loop(0, COL_DEV // TILE)
    def _(tile):
        cols = pl.ds(pl.multiple_of(tile * TILE, TILE), TILE)
        screen = dot(flat_ref[...], table_ref[:, cols]).astype(BF16).astype(F32)
        live = coherent_ref[:, cols].astype(F32)
        corrected_ref[:, cols] = (live * (series_ref[:, cols] - screen)).astype(BF16)


def vmem(count):
    return [pl.BlockSpec(memory_space=pltpu.VMEM)] * count


def anywhere(count):
    return [pl.BlockSpec(memory_space=pl.ANY)] * count


def per_device(phases, incidence, coherent):
    ifgs = phases.shape[0]

    series, trend_fit, spectrum, table = pl.pallas_call(
        series_kernel,
        out_shape=(
            jax.ShapeDtypeStruct((DATES, COL_DEV), F32),
            jax.ShapeDtypeStruct((2, 1, COL_DEV), F32),
            jax.ShapeDtypeStruct((PLANE, 32, 128), BF16),
            jax.ShapeDtypeStruct((2 * FREQS, COL_DEV), BF16),
        ),
        in_specs=vmem(3) + anywhere(1),
        out_specs=tuple(vmem(4)),
        scratch_shapes=[
            pltpu.VMEM((ifgs, COL_DEV), BF16),
            pltpu.VMEM((DATES, ifgs), BF16),
            pltpu.VMEM((DATES, 2 * FREQS), F32),
            pltpu.SemaphoreType.DMA,
        ],
        compiler_params=pltpu.CompilerParams(vmem_limit_bytes=40 * 2**20),
        name="series",
    )(incidence.T, coherent, jnp.asarray(angle_tables()), phases.reshape(ifgs, COL_DEV))

    weights = pl.pallas_call(
        exchange_kernel,
        out_shape=jax.ShapeDtypeStruct((PLANE, 32, 128), BF16),
        in_specs=vmem(3),
        out_specs=vmem(1)[0],
        scratch_shapes=[
            pltpu.VMEM((PLANE, 32, 128), BF16),
            pltpu.VMEM((DEPTH, 16, 128), BF16),
            pltpu.VMEM((DEPTH, 16, 128), BF16),
            pltpu.VMEM((DEPTH, 16, 128), BF16),
            pltpu.VMEM((DEPTH, 16, 128), BF16),
            pltpu.VMEM((SHELF, 32, 128), BF16),
            pltpu.VMEM((PLANE, 32, 128), BF16),
        ]
        + [
            pltpu.SemaphoreType.DMA((size,))
            for size in (PLANE, PLANE, DEPTH, DEPTH, DEPTH, DEPTH, PLANE, PLANE)
        ],
        compiler_params=pltpu.CompilerParams(
            collective_id=0, has_side_effects=True, vmem_limit_bytes=32 * 2**20
        ),
        name="exchange",
    )(
        spectrum,
        jnp.asarray(smoothing_matrix()),
        jnp.asarray(column_scales()),
    )

    corrected = pl.pallas_call(
        correct_kernel,
        out_shape=jax.ShapeDtypeStruct((DATES, COL_DEV), BF16),
        in_specs=vmem(4),
        out_specs=vmem(1)[0],
        scratch_shapes=[pltpu.VMEM((DATES, 2 * FREQS), BF16)],
        compiler_params=pltpu.CompilerParams(vmem_limit_bytes=40 * 2**20),
        name="correct",
    )(coherent, series, weights, table)

    return (corrected.reshape(DATES, 1, COL_DEV), trend_fit)


def solution(mesh):
    placed = (P(None, "grp", ("section", "sub")), P(), P("grp", ("section", "sub")))
    return jax.shard_map(
        per_device,
        mesh=mesh,
        in_specs=placed,
        out_specs=(P(None, "grp", ("section", "sub")), P(None, "grp", ("section", "sub"))),
        check_vma=False,
    )
```

```python
import math

import jax
import jax.numpy as jnp
import numpy as np
from jax import lax
from jax.experimental import pallas as pl
from jax.experimental.pallas import tpu as pltpu
from jax.sharding import PartitionSpec as P

MESH = pl.DeviceIdType.MESH
F32 = jnp.float32
BF16 = jnp.bfloat16

REG = 0.1
FREQS = 256
DATES = 256
ROWS = 128
COLS = 8192
BLOCKS = DATES // 8
COL_DEV = 2048
TILE = 512

PLANE = 32
DEPTH = 16
SHELF = 8


def angle_tables():
    frequency = np.arange(FREQS, dtype=np.int64)[:, None]
    column = np.arange(128, dtype=np.int64)[None, :]
    start = (frequency * column % COLS) * (2.0 * math.pi / COLS)
    step = (frequency * np.full_like(column, 128) % COLS) * (2.0 * math.pi / COLS)
    return np.stack([np.cos(start), np.sin(start), np.cos(step), np.sin(step)]).astype(np.float32)


def row_filter():
    indices = np.arange(ROWS)
    frequency = np.minimum(indices, ROWS - indices).astype(np.float64)
    taper = np.exp(-np.square(frequency / (ROWS / 4.0)))
    turns = (indices[:, None] * indices[None, :] % ROWS) * (2.0 * math.pi / ROWS)
    cos_rows, sin_rows = np.cos(turns), np.sin(turns)
    return ((cos_rows * taper) @ cos_rows.T + (sin_rows * taper) @ sin_rows.T) / ROWS


def smoothing_matrix():
    index = np.arange(DEPTH * SHELF * 2)
    z, shelf, half = index // 16, index // 2 % 8, index % 2
    row = shelf // 4 * 64 + z * 4 + shelf % 4
    full = row_filter()[row[:, None], row[None, :]] * (half[:, None] == half[None, :])
    return full.astype(np.float32)


def column_scales():
    frequency = np.arange(FREQS)
    scale = np.where(frequency == 0, 1.0, 2.0) * np.exp(-np.square(frequency / FREQS)) / COLS
    return scale.astype(np.float32).reshape(2, 1, 128)


def iota(shape, axis):
    return lax.broadcasted_iota(jnp.int32, shape, axis)


def hot(condition):
    return jnp.where(condition, 1.0, 0.0).astype(F32)


def dot(a, b):
    return jnp.dot(a, b, preferred_element_type=F32)


def dot_nt(a, b):
    return lax.dot_general(a, b, (((1,), (1,)), ((), ())), preferred_element_type=F32)


def lane_roll(x, shift):
    flat = x.reshape(64, 128)
    return pltpu.roll(flat, shift, 1).reshape(8, 8, 128)


def block_product(a, b):
    total = a[:, 0:1, :] * b[0][None]
    for k in range(1, 8):
        total = total + a[:, k : k + 1, :] * b[k][None]
    return total


def reciprocal(x):
    guess = pl.reciprocal(x, approx=True)
    guess = guess * (2.0 - x * guess)
    return guess * (2.0 - x * guess)


def block_inverse(d):
    sub = iota((8, 128), 0)
    rows = [d[i] for i in range(8)]
    for k in range(8):
        pivot = reciprocal(rows[k][k : k + 1, :])
        pivot_row = jnp.where(sub == k, pivot, rows[k] * pivot)
        for i in range(8):
            if i != k:
                factor = rows[i][k : k + 1, :]
                rows[i] = jnp.where(sub == k, 0.0, rows[i]) - factor * pivot_row
        rows[k] = pivot_row
    return jnp.stack(rows)


def split(x):
    high = x.astype(BF16)
    rest = x - high.astype(F32)
    middle = rest.astype(BF16)
    return high, middle, (rest - middle.astype(F32)).astype(BF16)


def dot_split(a, b):
    (ah, am, al), (bh, bm, bl) = a, b
    return dot(
        jnp.concatenate([al, am, ah, am, ah, ah], axis=1),
        jnp.concatenate([bh, bm, bl, bh, bm, bh], axis=0),
    )


def pseudo_inverse(incidence):
    count = incidence.shape[1]
    primary, secondary = incidence[0:1, :], incidence[1:2, :]
    dates = iota((DATES, count), 0)
    design_t = hot(dates == secondary) - hot(dates == primary)
    p_in, p_block, s_in, s_block = primary & 7, primary >> 3, secondary & 7, secondary >> 3
    block = iota((128, count), 0) & (BLOCKS - 1)
    at_primary = hot(block == p_block).astype(BF16)
    at_secondary = hot(block == s_block).astype(BF16)
    pair = iota((64, count), 0)
    same = hot(p_block == s_block)
    ps = hot(pair == p_in * 8 + s_in)
    sp = hot(pair == s_in * 8 + p_in)
    on_primary = hot(pair == p_in * 9) - same * (ps + sp)
    on_secondary = hot(pair == s_in * 9)
    to_next = (same - 1.0) * ps
    to_last = (same - 1.0) * sp
    from_primary = dot_nt(jnp.concatenate([on_primary, to_next], 0).astype(BF16), at_primary)
    from_secondary = dot_nt(jnp.concatenate([on_secondary, to_last], 0).astype(BF16), at_secondary)
    entry = iota((64, 128), 0)
    eye = hot((entry >> 3) == (entry & 7))
    diag = (from_primary[:64] + from_secondary[:64] + REG * eye).reshape(8, 8, 128)
    below = from_secondary[64:].reshape(8, 8, 128)
    above = from_primary[64:].reshape(8, 8, 128)
    first = (iota((8, 8, 128), 2) & BLOCKS) == 0

    date = iota((2 * DATES, 128), 0)
    take = hot((date >> 3) == iota((2 * DATES, 128), 1)).astype(BF16)
    own_row = ((iota((2 * DATES, 192), 1) >> 3) & 7) == (iota((2 * DATES, 192), 0) & 7)
    spread = hot((iota((192, DATES), 1) & 7) == (iota((192, DATES), 0) & 7)).astype(BF16)
    row_block = iota((DATES, DATES), 0) >> 3
    col_block = iota((DATES, DATES), 1) >> 3

    def blocks_of(x, sides):
        count = sides * DATES
        terms = jnp.concatenate(split(x.reshape(64, 128)), axis=0)
        rows = jnp.where(own_row[:count], dot_nt(take[:count], terms), 0.0).astype(BF16)
        return dot(rows, spread)

    total = None
    step = 1
    while step < BLOCKS:
        inverse = block_inverse(diag)
        near = jnp.where(first, lane_roll(inverse, step), lane_roll(inverse, 128 - step))
        gain = block_product(jnp.where(first, below, above), near)
        back = jnp.where(first, lane_roll(above, step), lane_roll(below, 128 - step))
        change = block_product(gain, back)
        diag = diag - change - lane_roll(change, BLOCKS)
        sides = blocks_of(gain, 2)
        gamma = jnp.where(
            col_block == row_block - step,
            sides[:DATES],
            jnp.where(col_block == row_block + step, sides[DATES:], 0.0),
        )
        if total is None:
            total = hot(iota((DATES, DATES), 0) == iota((DATES, DATES), 1)) - gamma
        else:
            total = total - dot_split(split(gamma), split(total))
        if 2 * step < BLOCKS:
            far = jnp.where(first, lane_roll(below, step), lane_roll(above, 128 - step))
            links = -block_product(gain, far)
            swapped = lane_roll(links, BLOCKS)
            below = jnp.where(first, links, swapped)
            above = jnp.where(first, swapped, links)
        step *= 2
    final = jnp.where(col_block == row_block, blocks_of(block_inverse(diag), 1), 0.0)
    inverse = dot_split(split(final), split(total))
    design_t = design_t.astype(BF16)
    return dot(
        jnp.concatenate(split(inverse)[::-1], axis=1),
        jnp.concatenate([design_t, design_t, design_t], axis=0),
    ).astype(BF16)


def part_index():
    return lax.axis_index("section") * 2 + lax.axis_index("sub")


def fill_table(angles_ref, table_ref):
    @pl.loop(0, FREQS // 16)
    def _(group):
        first = pl.multiple_of(group * 16, 16)
        rows, sin_rows = pl.ds(first, 16), pl.ds(first + FREQS, 16)
        cos, sin = angles_ref[0, rows, :], angles_ref[1, rows, :]
        step_cos, step_sin = angles_ref[2, rows, :], angles_ref[3, rows, :]
        quarter = ((iota((16, 128), 0) + first) * part_index()) & 3
        odd, minus = (quarter & 1) == 1, quarter >= 2
        cos, sin = jnp.where(odd, -sin, cos), jnp.where(odd, cos, sin)
        cos, sin = jnp.where(minus, -cos, cos), jnp.where(minus, -sin, sin)
        for tile in range(COL_DEV // 128):
            cols = slice(tile * 128, tile * 128 + 128)
            table_ref[rows, cols] = cos.astype(BF16)
            table_ref[sin_rows, cols] = (-sin).astype(BF16)
            cos, sin = cos * step_cos - sin * step_sin, sin * step_cos + cos * step_sin


def regroup_matrix(inverse):
    out, source = iota((256, 256), 0), iota((256, 256), 1)
    if inverse:
        out, source = source, out
    return hot(source == ((out >> 1) & 7) * 32 + (out >> 4) * 2 + (out & 1)).astype(BF16)


def screen_kernel(
    incidence_hbm,
    coherent_hbm,
    angles_hbm,
    smooth_hbm,
    scale_hbm,
    phases_hbm,
    corrected_hbm,
    trend_hbm,
    incidence_ref,
    coherent_ref,
    angles_ref,
    smooth_ref,
    scale_ref,
    phases_ref,
    corrected_ref,
    trend_ref,
    table_ref,
    series_ref,
    map_ref,
    total_ref,
    part_out,
    part_in,
    up_out,
    up_in,
    down_out,
    down_in,
    back_out,
    back_in,
    flat_ref,
    load_sems,
    store_sems,
    send_sems,
    recv_sems,
):
    loads = [
        pltpu.make_async_copy(source, target, load_sems.at[i])
        for i, (source, target) in enumerate(
            [
                (incidence_hbm, incidence_ref),
                (angles_hbm, angles_ref),
                (coherent_hbm, coherent_ref),
                (phases_hbm, phases_ref),
                (smooth_hbm, smooth_ref),
                (scale_hbm, scale_ref),
            ]
        )
    ]
    for load in loads:
        load.start()

    section, grp, sub = (lax.axis_index(name) for name in ("section", "grp", "sub"))
    y, z, x = grp // 64, grp // 4 % 16, grp % 4
    me = (section * 2 + sub) * 8 + y * 4 + x
    sections, subs, ys = (section, 1 - section), (sub, 1 - sub), (y, 1 - y)
    xs = [(x + hop) % 4 for hop in range(4)]
    zs = [(z + hop) % 16 for hop in range(16)]
    plane = [
        ((a * 2 + b) * 8 + c * 4 + d, c * 4 + d, (a, c * 64 + z * 4 + d, b))
        for d in xs
        for c in ys
        for b in subs
        for a in sections
    ][1:]
    column = [(other, other, (section, y * 64 + other * 4 + x, sub)) for other in zs][1:]

    barrier = pltpu.get_barrier_semaphore()
    for _, _, device in plane + column:
        pl.semaphore_signal(barrier, inc=1, device_id=device, device_id_type=MESH)

    loads[1].wait()
    fill_table(angles_ref, table_ref)
    loads[0].wait()
    map_ref[...] = pseudo_inverse(incidence_ref[...])
    total_ref[...] = jnp.zeros_like(total_ref)
    epochs = (2.0 * iota((DATES, 1), 0).astype(F32) - (DATES - 1)) / (DATES - 1)
    spread = sum(((2.0 * n - (DATES - 1)) / (DATES - 1)) ** 2 for n in range(DATES))
    for load in loads[2:]:
        load.wait()

    @pl.loop(0, COL_DEV // TILE)
    def _(tile):
        cols = pl.ds(pl.multiple_of(tile * TILE, TILE), TILE)
        series = dot(map_ref[...], phases_ref[:, cols])
        series_ref[:, cols] = series
        offset = jnp.sum(series, axis=0, keepdims=True) / DATES
        rate = jnp.sum(epochs * series, axis=0, keepdims=True) / spread
        trend_ref[0, :, cols] = offset
        trend_ref[1, :, cols] = rate
        live = coherent_ref[:, cols].astype(F32)
        residual = (live * (series - offset - epochs * rate)).astype(BF16)
        total_ref[...] += dot_nt(residual, table_ref[:, cols])

    for nb in range(8):
        for jb in range(4):
            part_out[nb * 4 + jb] = total_ref[
                nb * 32 : nb * 32 + 32, jb * 128 : jb * 128 + 128
            ].astype(BF16)

    trend_store = pltpu.make_async_copy(trend_ref, trend_hbm, store_sems.at[COL_DEV // TILE])
    trend_store.start()
    pl.semaphore_wait(barrier, len(plane) + len(column))

    def exchange(phase, mine, partners, source, target):
        for other, row, device in partners:
            pltpu.make_async_remote_copy(
                src_ref=source(other, row),
                dst_ref=target.at[mine],
                send_sem=send_sems.at[phase],
                recv_sem=recv_sems.at[phase],
                device_id=device,
                device_id_type=MESH,
            ).start()
        target[mine] = source(mine, lax.rem(mine, SHELF))[...]

    def arrived(phase, target, sems):
        blocks = target.at[pl.ds(0, target.shape[0] - 1)]
        pltpu.make_async_copy(blocks, blocks, sems.at[phase]).wait()

    exchange(0, me, plane, lambda other, row: part_out.at[other], part_in)
    smooth = smooth_ref[...]
    smooth_high = smooth.astype(BF16)
    smooth_low = (smooth - smooth_high.astype(F32)).astype(BF16)
    regroup, ungroup = regroup_matrix(False), regroup_matrix(True)
    arrived(0, part_in, recv_sems)
    row_sum = jnp.sum(part_in[...].astype(F32).reshape(4, 256, 128), axis=0).astype(BF16)
    up_out[...] = dot(regroup, row_sum).astype(BF16).reshape(DEPTH, 16, 128)
    exchange(1, z, column, lambda other, row: up_out.at[other], up_in)
    arrived(1, up_in, recv_sems)
    rows = up_in[...].reshape(256, 128)
    smoothed = dot(smooth_high, rows) + dot(smooth_low, rows)
    down_out[...] = (smoothed * scale_ref[me % 2]).astype(BF16).reshape(DEPTH, 16, 128)
    exchange(2, z, column, lambda other, row: down_out.at[other], down_in)
    arrived(2, down_in, recv_sems)
    whole = down_in[...].reshape(256, 128)
    back_out[...] = dot(ungroup, whole).astype(BF16).reshape(SHELF, 32, 128)
    exchange(3, me, plane, lambda other, row: back_out.at[row], back_in)
    arrived(3, back_in, recv_sems)

    for nb in range(8):
        for jb in range(4):
            flat_ref[nb * 32 : nb * 32 + 32, jb * 128 : jb * 128 + 128] = back_in[nb * 4 + jb]

    def store(tile):
        cols = pl.ds(pl.multiple_of(tile * TILE, TILE), TILE)
        return pltpu.make_async_copy(
            corrected_ref.at[:, cols], corrected_hbm.at[:, cols], store_sems.at[tile]
        )

    @pl.loop(0, COL_DEV // TILE)
    def _(tile):
        cols = pl.ds(pl.multiple_of(tile * TILE, TILE), TILE)
        screen = dot(flat_ref[...], table_ref[:, cols]).astype(BF16).astype(F32)
        live = coherent_ref[:, cols].astype(F32)
        corrected_ref[:, cols] = (live * (series_ref[:, cols] - screen)).astype(BF16)
        store(tile).start()

    arrived(0, part_in, send_sems)
    arrived(1, up_in, send_sems)
    arrived(2, down_in, send_sems)
    arrived(3, back_in, send_sems)
    trend_store.wait()

    @pl.loop(0, COL_DEV // TILE)
    def _(tile):
        store(tile).wait()


def per_device(phases, incidence, coherent):
    ifgs = phases.shape[0]
    anywhere = pl.BlockSpec(memory_space=pl.ANY)
    corrected, trend_fit = pl.pallas_call(
        screen_kernel,
        out_shape=(
            jax.ShapeDtypeStruct((DATES, COL_DEV), BF16),
            jax.ShapeDtypeStruct((2, 1, COL_DEV), F32),
        ),
        in_specs=[anywhere] * 6,
        out_specs=(anywhere, anywhere),
        scratch_shapes=[
            pltpu.VMEM((2, ifgs), jnp.int32),
            pltpu.VMEM((1, COL_DEV), jnp.int32),
            pltpu.VMEM((4, FREQS, 128), F32),
            pltpu.VMEM((256, 256), F32),
            pltpu.VMEM((2, 1, 128), F32),
            pltpu.VMEM((ifgs, COL_DEV), BF16),
            pltpu.VMEM((DATES, COL_DEV), BF16),
            pltpu.VMEM((2, 1, COL_DEV), F32),
            pltpu.VMEM((2 * FREQS, COL_DEV), BF16),
            pltpu.VMEM((DATES, COL_DEV), F32),
            pltpu.VMEM((DATES, ifgs), BF16),
            pltpu.VMEM((DATES, 2 * FREQS), F32),
            pltpu.VMEM((PLANE, 32, 128), BF16),
            pltpu.VMEM((PLANE, 32, 128), BF16),
            pltpu.VMEM((DEPTH, 16, 128), BF16),
            pltpu.VMEM((DEPTH, 16, 128), BF16),
            pltpu.VMEM((DEPTH, 16, 128), BF16),
            pltpu.VMEM((DEPTH, 16, 128), BF16),
            pltpu.VMEM((SHELF, 32, 128), BF16),
            pltpu.VMEM((PLANE, 32, 128), BF16),
            pltpu.VMEM((DATES, 2 * FREQS), BF16),
            pltpu.SemaphoreType.DMA((6,)),
            pltpu.SemaphoreType.DMA((COL_DEV // TILE + 1,)),
            pltpu.SemaphoreType.DMA((4,)),
            pltpu.SemaphoreType.DMA((4,)),
        ],
        compiler_params=pltpu.CompilerParams(
            collective_id=0, has_side_effects=True, vmem_limit_bytes=64 * 2**20
        ),
        name="screen",
    )(
        incidence.T,
        coherent,
        jnp.asarray(angle_tables()),
        jnp.asarray(smoothing_matrix()),
        jnp.asarray(column_scales()),
        phases.reshape(ifgs, COL_DEV),
    )
    return (corrected.reshape(DATES, 1, COL_DEV), trend_fit)


def solution(mesh):
    placed = (P(None, "grp", ("section", "sub")), P(), P("grp", ("section", "sub")))
    return jax.shard_map(
        per_device,
        mesh=mesh,
        in_specs=placed,
        out_specs=(P(None, "grp", ("section", "sub")), P(None, "grp", ("section", "sub"))),
        check_vma=False,
    )
```

```python
import math

import jax
import jax.numpy as jnp
import numpy as np
from jax import lax
from jax.experimental import pallas as pl
from jax.experimental.pallas import tpu as pltpu
from jax.sharding import PartitionSpec as P

MESH = pl.DeviceIdType.MESH
F32 = jnp.float32
BF16 = jnp.bfloat16

REG = 0.1
FREQS = 256
DATES = 256
ROWS = 128
COLS = 8192
BLOCKS = DATES // 8
COL_DEV = 2048
TILE = 512

PLANE = 16
HALF = DATES // 2
DEPTH = 16
SHELF = 8


def angle_tables():
    frequency = np.arange(FREQS, dtype=np.int64)[:, None]
    column = np.arange(128, dtype=np.int64)[None, :]
    start = (frequency * column % COLS) * (2.0 * math.pi / COLS)
    step = (frequency * np.full_like(column, 128) % COLS) * (2.0 * math.pi / COLS)
    return np.stack([np.cos(start), np.sin(start), np.cos(step), np.sin(step)]).astype(np.float32)


def row_filter():
    indices = np.arange(ROWS)
    frequency = np.minimum(indices, ROWS - indices).astype(np.float64)
    taper = np.exp(-np.square(frequency / (ROWS / 4.0)))
    turns = (indices[:, None] * indices[None, :] % ROWS) * (2.0 * math.pi / ROWS)
    cos_rows, sin_rows = np.cos(turns), np.sin(turns)
    return ((cos_rows * taper) @ cos_rows.T + (sin_rows * taper) @ sin_rows.T) / ROWS


def smoothing_matrix():
    index = np.arange(DEPTH * SHELF * 2)
    z, shelf, half = index // 16, index // 2 % 8, index % 2
    row = shelf // 4 * 64 + z * 4 + shelf % 4
    full = row_filter()[row[:, None], row[None, :]] * (half[:, None] == half[None, :])
    return full.astype(np.float32)


def column_scales():
    frequency = np.arange(FREQS)
    scale = np.where(frequency == 0, 1.0, 2.0) * np.exp(-np.square(frequency / FREQS)) / COLS
    return scale.astype(np.float32).reshape(2, 1, 128)


def iota(shape, axis):
    return lax.broadcasted_iota(jnp.int32, shape, axis)


def hot(condition):
    return jnp.where(condition, 1.0, 0.0).astype(F32)


def dot(a, b):
    return jnp.dot(a, b, preferred_element_type=F32)


def dot_nt(a, b):
    return lax.dot_general(a, b, (((1,), (1,)), ((), ())), preferred_element_type=F32)


def lane_roll(x, shift):
    flat = x.reshape(64, 128)
    return pltpu.roll(flat, shift, 1).reshape(8, 8, 128)


def block_product(a, b):
    total = a[:, 0:1, :] * b[0][None]
    for k in range(1, 8):
        total = total + a[:, k : k + 1, :] * b[k][None]
    return total


def reciprocal(x):
    guess = pl.reciprocal(x, approx=True)
    guess = guess * (2.0 - x * guess)
    return guess * (2.0 - x * guess)


def block_inverse(d):
    sub = iota((8, 128), 0)
    rows = [d[i] for i in range(8)]
    for k in range(8):
        pivot = reciprocal(rows[k][k : k + 1, :])
        pivot_row = jnp.where(sub == k, pivot, rows[k] * pivot)
        for i in range(8):
            if i != k:
                factor = rows[i][k : k + 1, :]
                rows[i] = jnp.where(sub == k, 0.0, rows[i]) - factor * pivot_row
        rows[k] = pivot_row
    return jnp.stack(rows)


def split(x):
    high = x.astype(BF16)
    rest = x - high.astype(F32)
    middle = rest.astype(BF16)
    return high, middle, (rest - middle.astype(F32)).astype(BF16)


def dot_split(a, b):
    (ah, am, al), (bh, bm, bl) = a, b
    return dot(
        jnp.concatenate([al, am, ah, am, ah, ah], axis=1),
        jnp.concatenate([bh, bm, bl, bh, bm, bh], axis=0),
    )


def pseudo_inverse(incidence):
    count = incidence.shape[1]
    primary, secondary = incidence[0:1, :], incidence[1:2, :]
    dates = iota((DATES, count), 0)
    design_t = hot(dates == secondary) - hot(dates == primary)
    p_in, p_block, s_in, s_block = primary & 7, primary >> 3, secondary & 7, secondary >> 3
    block = iota((128, count), 0) & (BLOCKS - 1)
    at_primary = hot(block == p_block).astype(BF16)
    at_secondary = hot(block == s_block).astype(BF16)
    pair = iota((64, count), 0)
    same = hot(p_block == s_block)
    ps = hot(pair == p_in * 8 + s_in)
    sp = hot(pair == s_in * 8 + p_in)
    on_primary = hot(pair == p_in * 9) - same * (ps + sp)
    on_secondary = hot(pair == s_in * 9)
    to_next = (same - 1.0) * ps
    to_last = (same - 1.0) * sp
    from_primary = dot_nt(jnp.concatenate([on_primary, to_next], 0).astype(BF16), at_primary)
    from_secondary = dot_nt(jnp.concatenate([on_secondary, to_last], 0).astype(BF16), at_secondary)
    entry = iota((64, 128), 0)
    eye = hot((entry >> 3) == (entry & 7))
    diag = (from_primary[:64] + from_secondary[:64] + REG * eye).reshape(8, 8, 128)
    below = from_secondary[64:].reshape(8, 8, 128)
    above = from_primary[64:].reshape(8, 8, 128)
    first = (iota((8, 8, 128), 2) & BLOCKS) == 0

    date = iota((2 * DATES, 128), 0)
    take = hot((date >> 3) == iota((2 * DATES, 128), 1)).astype(BF16)
    own_row = ((iota((2 * DATES, 192), 1) >> 3) & 7) == (iota((2 * DATES, 192), 0) & 7)
    spread = hot((iota((192, DATES), 1) & 7) == (iota((192, DATES), 0) & 7)).astype(BF16)
    row_block = iota((DATES, DATES), 0) >> 3
    col_block = iota((DATES, DATES), 1) >> 3

    def blocks_of(x, sides):
        count = sides * DATES
        terms = jnp.concatenate(split(x.reshape(64, 128)), axis=0)
        rows = jnp.where(own_row[:count], dot_nt(take[:count], terms), 0.0).astype(BF16)
        return dot(rows, spread)

    total = None
    step = 1
    while step < BLOCKS:
        inverse = block_inverse(diag)
        near = jnp.where(first, lane_roll(inverse, step), lane_roll(inverse, 128 - step))
        gain = block_product(jnp.where(first, below, above), near)
        back = jnp.where(first, lane_roll(above, step), lane_roll(below, 128 - step))
        change = block_product(gain, back)
        diag = diag - change - lane_roll(change, BLOCKS)
        sides = blocks_of(gain, 2)
        gamma = jnp.where(
            col_block == row_block - step,
            sides[:DATES],
            jnp.where(col_block == row_block + step, sides[DATES:], 0.0),
        )
        if total is None:
            total = hot(iota((DATES, DATES), 0) == iota((DATES, DATES), 1)) - gamma
        else:
            total = total - dot_split(split(gamma), split(total))
        if 2 * step < BLOCKS:
            far = jnp.where(first, lane_roll(below, step), lane_roll(above, 128 - step))
            links = -block_product(gain, far)
            swapped = lane_roll(links, BLOCKS)
            below = jnp.where(first, links, swapped)
            above = jnp.where(first, swapped, links)
        step *= 2
    final = jnp.where(col_block == row_block, blocks_of(block_inverse(diag), 1), 0.0)
    inverse = dot_split(split(final), split(total))
    design_t = design_t.astype(BF16)
    return dot(
        jnp.concatenate(split(inverse)[::-1], axis=1),
        jnp.concatenate([design_t, design_t, design_t], axis=0),
    ).astype(BF16)


def part_index():
    return lax.axis_index("section") * 2 + lax.axis_index("sub")


def fill_table(angles_ref, table_ref):
    @pl.loop(0, FREQS // 64)
    def _(group):
        first = pl.multiple_of(group * 64, 64)
        rows, sin_rows = pl.ds(first, 64), pl.ds(first + FREQS, 64)
        cos, sin = angles_ref[0, rows, :], angles_ref[1, rows, :]
        step_cos, step_sin = angles_ref[2, rows, :], angles_ref[3, rows, :]
        quarter = ((iota((64, 128), 0) + first) * part_index()) & 3
        odd, minus = (quarter & 1) == 1, quarter >= 2
        cos, sin = jnp.where(odd, -sin, cos), jnp.where(odd, cos, sin)
        cos, sin = jnp.where(minus, -cos, cos), jnp.where(minus, -sin, sin)
        for tile in range(COL_DEV // 128):
            cols = slice(tile * 128, tile * 128 + 128)
            table_ref[rows, cols] = cos.astype(BF16)
            table_ref[sin_rows, cols] = (-sin).astype(BF16)
            cos, sin = cos * step_cos - sin * step_sin, sin * step_cos + cos * step_sin


def regroup_matrix(inverse):
    out, source = iota((256, 256), 0), iota((256, 256), 1)
    if inverse:
        out, source = source, out
    return hot(source == ((out >> 1) & 7) * 32 + (out >> 4) * 2 + (out & 1)).astype(BF16)


def screen_kernel(
    incidence_hbm,
    coherent_hbm,
    angles_hbm,
    smooth_hbm,
    scale_hbm,
    phases_hbm,
    corrected_ref,
    trend_ref,
    incidence_ref,
    coherent_ref,
    angles_ref,
    smooth_ref,
    scale_ref,
    phases_ref,
    table_ref,
    series_ref,
    residual_ref,
    map_ref,
    pair_out,
    pair_in,
    part_out,
    part_in,
    up_out,
    up_in,
    down_out,
    down_in,
    back_out,
    back_in,
    swap_in,
    flat_ref,
    load_sems,
    send_sems,
    recv_sems,
):
    loads = [
        pltpu.make_async_copy(source, target, load_sems.at[i])
        for i, (source, target) in enumerate(
            [
                (incidence_hbm, incidence_ref),
                (angles_hbm, angles_ref),
                (coherent_hbm, coherent_ref),
                (phases_hbm, phases_ref),
                (smooth_hbm, smooth_ref),
                (scale_hbm, scale_ref),
            ]
        )
    ]
    for load in loads:
        load.start()

    section, grp, sub = (lax.axis_index(name) for name in ("section", "grp", "sub"))
    y, z, x = grp // 64, grp // 4 % 16, grp % 4
    me = sub * 8 + y * 4 + x
    subs, ys = (sub, 1 - sub), (y, 1 - y)
    xs = [(x + hop) % 4 for hop in (2, 1, 3, 0)]
    zs = [(z + hop) % 16 for hop in (8, 7, 9, 6, 10, 5, 11, 4, 12, 3, 13, 2, 14, 1, 15)]
    plane = [
        (b * 8 + c * 4 + d, c * 4 + d, (section, c * 64 + z * 4 + d, b))
        for d in xs
        for b in subs[::-1]
        for c in ys[::-1]
    ][:-1]
    column = [(other, other, (section, y * 64 + other * 4 + x, sub)) for other in zs]
    partner = (1 - section, grp, sub)

    barrier = pltpu.get_barrier_semaphore()
    for device in [partner] + [device for _, _, device in plane + column]:
        pl.semaphore_signal(barrier, inc=1, device_id=device, device_id_type=MESH)

    loads[1].wait()
    fill_table(angles_ref, table_ref)
    loads[0].wait()
    map_ref[...] = pseudo_inverse(incidence_ref[...])
    epochs = (2.0 * iota((DATES, 1), 0).astype(F32) - (DATES - 1)) / (DATES - 1)
    spread = sum(((2.0 * n - (DATES - 1)) / (DATES - 1)) ** 2 for n in range(DATES))
    for load in loads[2:]:
        load.wait()

    for tile in range(COL_DEV // TILE):
        cols = slice(tile * TILE, tile * TILE + TILE)
        series = dot(map_ref[...], phases_ref[:, cols])
        series_ref[:, cols] = series
        offset = jnp.sum(series, axis=0, keepdims=True) / DATES
        rate = jnp.sum(epochs * series, axis=0, keepdims=True) / spread
        trend_ref[0, :, cols] = offset
        trend_ref[1, :, cols] = rate
        live = coherent_ref[:, cols].astype(F32)
        residual_ref[:, cols] = (live * (series - offset - epochs * rate)).astype(BF16)

    def half_rows(half):
        return pl.ds(pl.multiple_of(half * HALF, HALF), HALF)

    def block(array, number):
        row, col = number // 4 * 32, number % 4 * 128
        return array[row : row + 32, col : col + 128]

    pl.semaphore_wait(barrier, 1 + len(plane) + len(column))

    theirs = dot_nt(residual_ref[half_rows(1 - section), :], table_ref[...]).astype(BF16)
    for number in range(PLANE):
        pair_out[number] = block(theirs, number)
    give = pltpu.make_async_remote_copy(
        src_ref=pair_out,
        dst_ref=pair_in,
        send_sem=send_sems.at[4],
        recv_sem=recv_sems.at[4],
        device_id=partner,
        device_id_type=MESH,
    )
    give.start()
    ours = dot_nt(residual_ref[half_rows(section), :], table_ref[...])
    give.wait_recv()
    for number in range(PLANE):
        part_out[number] = (block(ours, number) + pair_in[number].astype(F32)).astype(BF16)

    def exchange(phase, mine, partners, source, target):
        for other, row, device in partners:
            pltpu.make_async_remote_copy(
                src_ref=source(other, row),
                dst_ref=target.at[mine],
                send_sem=send_sems.at[phase],
                recv_sem=recv_sems.at[phase],
                device_id=device,
                device_id_type=MESH,
            ).start()
        target[mine] = source(mine, lax.rem(mine, SHELF))[...]

    def arrived(phase, target, sems):
        blocks = target.at[pl.ds(0, target.shape[0] - 1)]
        pltpu.make_async_copy(blocks, blocks, sems.at[phase]).wait()

    exchange(0, me, plane, lambda other, row: part_out.at[other], part_in)
    smooth = smooth_ref[...]
    smooth_high = smooth.astype(BF16)
    smooth_low = (smooth - smooth_high.astype(F32)).astype(BF16)
    regroup, ungroup = regroup_matrix(False), regroup_matrix(True)
    arrived(0, part_in, recv_sems)
    row_sum = jnp.sum(part_in[...].astype(F32).reshape(2, 256, 128), axis=0).astype(BF16)
    up_out[...] = dot(regroup, row_sum).astype(BF16).reshape(DEPTH, 16, 128)
    exchange(1, z, column, lambda other, row: up_out.at[other], up_in)
    arrived(1, up_in, recv_sems)
    rows = up_in[...].reshape(256, 128)
    smoothed = dot(smooth_high, rows) + dot(smooth_low, rows)
    down_out[...] = (smoothed * scale_ref[me % 2]).astype(BF16).reshape(DEPTH, 16, 128)
    exchange(2, z, column, lambda other, row: down_out.at[other], down_in)
    arrived(2, down_in, recv_sems)
    whole = down_in[...].reshape(256, 128)
    back_out[...] = dot(ungroup, whole).astype(BF16).reshape(SHELF, 32, 128)
    exchange(3, me, plane, lambda other, row: back_out.at[row], back_in)
    arrived(3, back_in, recv_sems)

    swap = pltpu.make_async_remote_copy(
        src_ref=back_in,
        dst_ref=swap_in,
        send_sem=send_sems.at[5],
        recv_sem=recv_sems.at[5],
        device_id=partner,
        device_id_type=MESH,
    )
    swap.start()

    def correct(half, weights):
        for number in range(PLANE):
            row, col = number // 4 * 32, number % 4 * 128
            flat_ref[row : row + 32, col : col + 128] = weights[number]
        dates = half_rows(half)
        for tile in range(COL_DEV // TILE):
            cols = slice(tile * TILE, tile * TILE + TILE)
            screen = dot(flat_ref[...], table_ref[:, cols]).astype(BF16).astype(F32)
            live = coherent_ref[:, cols].astype(F32)
            corrected_ref[dates, cols] = (live * (series_ref[dates, cols] - screen)).astype(BF16)

    correct(section, back_in)
    give.wait_send()
    arrived(0, part_in, send_sems)
    arrived(1, up_in, send_sems)
    arrived(2, down_in, send_sems)
    arrived(3, back_in, send_sems)
    swap.wait_recv()
    correct(1 - section, swap_in)
    swap.wait_send()


def store_kernel(corrected_ref, trend_ref, corrected_hbm, trend_hbm, sems):
    stores = [
        pltpu.make_async_copy(corrected_ref, corrected_hbm, sems.at[0]),
        pltpu.make_async_copy(trend_ref, trend_hbm, sems.at[1]),
    ]
    for store in stores:
        store.start()
    for store in stores:
        store.wait()


def per_device(phases, incidence, coherent):
    ifgs = phases.shape[0]
    in_hbm = pl.BlockSpec(memory_space=pltpu.HBM)
    in_vmem = pl.BlockSpec(memory_space=pltpu.VMEM)
    results = (
        jax.ShapeDtypeStruct((DATES, COL_DEV), BF16),
        jax.ShapeDtypeStruct((2, 1, COL_DEV), F32),
    )
    operands = (
        incidence.T,
        coherent,
        jnp.asarray(angle_tables()),
        jnp.asarray(smoothing_matrix()),
        jnp.asarray(column_scales()),
        phases.reshape(ifgs, COL_DEV),
    )
    corrected, trend_fit = pl.pallas_call(
        screen_kernel,
        out_shape=results,
        in_specs=[in_hbm] * 6,
        out_specs=(in_vmem, in_vmem),
        scratch_shapes=[
            pltpu.VMEM((2, ifgs), jnp.int32),
            pltpu.VMEM((1, COL_DEV), jnp.int32),
            pltpu.VMEM((4, FREQS, 128), F32),
            pltpu.VMEM((256, 256), F32),
            pltpu.VMEM((2, 1, 128), F32),
            pltpu.VMEM((ifgs, COL_DEV), BF16),
            pltpu.VMEM((2 * FREQS, COL_DEV), BF16),
            pltpu.VMEM((DATES, COL_DEV), F32),
            pltpu.VMEM((DATES, COL_DEV), BF16),
            pltpu.VMEM((DATES, ifgs), BF16),
            pltpu.VMEM((PLANE, 32, 128), BF16),
            pltpu.VMEM((PLANE, 32, 128), BF16),
            pltpu.VMEM((PLANE, 32, 128), BF16),
            pltpu.VMEM((PLANE, 32, 128), BF16),
            pltpu.VMEM((DEPTH, 16, 128), BF16),
            pltpu.VMEM((DEPTH, 16, 128), BF16),
            pltpu.VMEM((DEPTH, 16, 128), BF16),
            pltpu.VMEM((DEPTH, 16, 128), BF16),
            pltpu.VMEM((SHELF, 32, 128), BF16),
            pltpu.VMEM((PLANE, 32, 128), BF16),
            pltpu.VMEM((PLANE, 32, 128), BF16),
            pltpu.VMEM((HALF, 2 * FREQS), BF16),
            pltpu.SemaphoreType.DMA((6,)),
            pltpu.SemaphoreType.DMA((6,)),
            pltpu.SemaphoreType.DMA((6,)),
        ],
        compiler_params=pltpu.CompilerParams(
            collective_id=0, has_side_effects=True, vmem_limit_bytes=36 * 2**20
        ),
        name="screen",
    )(*(pltpu.with_memory_space_constraint(operand, pltpu.HBM) for operand in operands))
    corrected, trend_fit = pl.pallas_call(
        store_kernel,
        out_shape=results,
        in_specs=[in_vmem] * 2,
        out_specs=(in_hbm, in_hbm),
        scratch_shapes=[pltpu.SemaphoreType.DMA((2,))],
        compiler_params=pltpu.CompilerParams(vmem_limit_bytes=8 * 2**20),
        name="store",
    )(corrected, trend_fit)
    return (corrected.reshape(DATES, 1, COL_DEV), trend_fit)


def solution(mesh):
    placed = (P(None, "grp", ("section", "sub")), P(), P("grp", ("section", "sub")))
    return jax.shard_map(
        per_device,
        mesh=mesh,
        in_specs=placed,
        out_specs=(P(None, "grp", ("section", "sub")), P(None, "grp", ("section", "sub"))),
        check_vma=False,
    )
```

```python
import functools
import math

import jax
import jax.numpy as jnp
import numpy as np
from jax import lax
from jax.experimental import pallas as pl
from jax.experimental.pallas import tpu as pltpu
from jax.sharding import PartitionSpec as P

MESH = pl.DeviceIdType.MESH
F32 = jnp.float32
BF16 = jnp.bfloat16

REG = 0.1
FREQS = 256
DATES = 256
ROWS = 128
COLS = 8192
BLOCKS = DATES // 8
COL_DEV = 2048
TILE = 512

PLANE = 16
HALF = DATES // 2
DEPTH = 16
SHELF = 8


def angle_tables():
    frequency = np.arange(FREQS, dtype=np.int64)[:, None]
    column = np.arange(128, dtype=np.int64)[None, :]
    start = (frequency * column % COLS) * (2.0 * math.pi / COLS)
    step = (frequency * np.full_like(column, 128) % COLS) * (2.0 * math.pi / COLS)
    return np.stack([np.cos(start), np.sin(start), np.cos(step), np.sin(step)]).astype(np.float32)


def row_filter():
    indices = np.arange(ROWS)
    frequency = np.minimum(indices, ROWS - indices).astype(np.float64)
    taper = np.exp(-np.square(frequency / (ROWS / 4.0)))
    turns = (indices[:, None] * indices[None, :] % ROWS) * (2.0 * math.pi / ROWS)
    cos_rows, sin_rows = np.cos(turns), np.sin(turns)
    return ((cos_rows * taper) @ cos_rows.T + (sin_rows * taper) @ sin_rows.T) / ROWS


def smoothing_matrix():
    index = np.arange(DEPTH * SHELF * 2)
    z, shelf, half = index // 16, index // 2 % 8, index % 2
    row = shelf // 4 * 64 + z * 4 + shelf % 4
    full = row_filter()[row[:, None], row[None, :]] * (half[:, None] == half[None, :])
    return full.astype(np.float32)


def column_scales():
    frequency = np.arange(FREQS)
    scale = np.where(frequency == 0, 1.0, 2.0) * np.exp(-np.square(frequency / FREQS)) / COLS
    return scale.astype(np.float32).reshape(2, 1, 128)


def iota(shape, axis):
    return lax.broadcasted_iota(jnp.int32, shape, axis)


def hot(condition):
    return jnp.where(condition, 1.0, 0.0).astype(F32)


def dot(a, b):
    return jnp.dot(a, b, preferred_element_type=F32)


def dot_nt(a, b):
    return lax.dot_general(a, b, (((1,), (1,)), ((), ())), preferred_element_type=F32)


def lane_roll(x, shift):
    flat = x.reshape(64, 128)
    return pltpu.roll(flat, shift, 1).reshape(8, 8, 128)


def block_product(a, b):
    terms = [a[:, k : k + 1, :] * b[k][None] for k in range(8)]
    while len(terms) > 1:
        terms = [one + two for one, two in zip(terms[::2], terms[1::2])]
    return terms[0]


def reciprocal(x):
    guess = pl.reciprocal(x, approx=True)
    guess = guess * (2.0 - x * guess)
    return guess * (2.0 - x * guess)


def block_inverse(d):
    sub = iota((8, 128), 0)
    rows = [d[i] for i in range(8)]
    for k in range(0, 8, 2):
        a, b = rows[k][k : k + 1, :], rows[k][k + 1 : k + 2, :]
        c, e = rows[k + 1][k : k + 1, :], rows[k + 1][k + 1 : k + 2, :]
        scale = reciprocal(a * e - b * c)
        one, two = sub == k, sub == k + 1
        first = jnp.where(one, 1.0, jnp.where(two, 0.0, rows[k]))
        second = jnp.where(one, 0.0, jnp.where(two, 1.0, rows[k + 1]))
        top = (e * scale) * first - (b * scale) * second
        bottom = (a * scale) * second - (c * scale) * first
        for i in range(8):
            if i not in (k, k + 1):
                f, g = rows[i][k : k + 1, :], rows[i][k + 1 : k + 2, :]
                rest = jnp.where(one | two, 0.0, rows[i])
                rows[i] = rest - (f * top + g * bottom)
        rows[k], rows[k + 1] = top, bottom
    return jnp.stack(rows)


def split(x):
    high = x.astype(BF16)
    rest = x - high.astype(F32)
    middle = rest.astype(BF16)
    return high, middle, (rest - middle.astype(F32)).astype(BF16)


def dot_split(a, b):
    (ah, am, al), (bh, bm, bl) = a, b
    return dot(
        jnp.concatenate([al, am, ah, am, ah, ah], axis=1),
        jnp.concatenate([bh, bm, bl, bh, bm, bh], axis=0),
    )


def pseudo_inverse(incidence, beside):
    count = incidence.shape[1]
    primary, secondary = incidence[0:1, :], incidence[1:2, :]
    dates = iota((DATES, count), 0)
    design_t = hot(dates == secondary) - hot(dates == primary)
    p_in, p_block, s_in, s_block = primary & 7, primary >> 3, secondary & 7, secondary >> 3
    block = iota((128, count), 0) & (BLOCKS - 1)
    at_primary = hot(block == p_block).astype(BF16)
    at_secondary = hot(block == s_block).astype(BF16)
    pair = iota((64, count), 0)
    same = hot(p_block == s_block)
    ps = hot(pair == p_in * 8 + s_in)
    sp = hot(pair == s_in * 8 + p_in)
    on_primary = hot(pair == p_in * 9) - same * (ps + sp)
    on_secondary = hot(pair == s_in * 9)
    to_next = (same - 1.0) * ps
    to_last = (same - 1.0) * sp
    from_primary = dot_nt(jnp.concatenate([on_primary, to_next], 0).astype(BF16), at_primary)
    from_secondary = dot_nt(jnp.concatenate([on_secondary, to_last], 0).astype(BF16), at_secondary)
    entry = iota((64, 128), 0)
    eye = hot((entry >> 3) == (entry & 7))
    diag = (from_primary[:64] + from_secondary[:64] + REG * eye).reshape(8, 8, 128)
    below = from_secondary[64:].reshape(8, 8, 128)
    above = from_primary[64:].reshape(8, 8, 128)
    first = (iota((8, 8, 128), 2) & BLOCKS) == 0

    date = iota((2 * DATES, 128), 0)
    take = hot((date >> 3) == iota((2 * DATES, 128), 1)).astype(BF16)
    own_row = ((iota((2 * DATES, 192), 1) >> 3) & 7) == (iota((2 * DATES, 192), 0) & 7)
    spread = hot((iota((192, DATES), 1) & 7) == (iota((192, DATES), 0) & 7)).astype(BF16)
    row_block = iota((DATES, DATES), 0) >> 3
    col_block = iota((DATES, DATES), 1) >> 3

    def blocks_of(x, sides):
        count = sides * DATES
        terms = jnp.concatenate(split(x.reshape(64, 128)), axis=0)
        rows = jnp.where(own_row[:count], dot_nt(take[:count], terms), 0.0).astype(BF16)
        return dot(rows, spread)

    total = None
    step = 1
    while step < BLOCKS:
        beside()
        inverse = block_inverse(diag)
        near = jnp.where(first, lane_roll(inverse, step), lane_roll(inverse, 128 - step))
        gain = block_product(jnp.where(first, below, above), near)
        back = jnp.where(first, lane_roll(above, step), lane_roll(below, 128 - step))
        change = block_product(gain, back)
        diag = diag - change - lane_roll(change, BLOCKS)
        sides = blocks_of(gain, 2)
        gamma = jnp.where(
            col_block == row_block - step,
            sides[:DATES],
            jnp.where(col_block == row_block + step, sides[DATES:], 0.0),
        )
        if total is None:
            total = hot(iota((DATES, DATES), 0) == iota((DATES, DATES), 1)) - gamma
        else:
            total = total - dot_split(split(gamma), split(total))
        if 2 * step < BLOCKS:
            far = jnp.where(first, lane_roll(below, step), lane_roll(above, 128 - step))
            links = -block_product(gain, far)
            swapped = lane_roll(links, BLOCKS)
            below = jnp.where(first, links, swapped)
            above = jnp.where(first, swapped, links)
        step *= 2
    design_t = design_t.astype(BF16)
    reduced = dot(
        jnp.concatenate(split(total)[::-1], axis=1),
        jnp.concatenate([design_t, design_t, design_t], axis=0),
    )
    final = jnp.where(col_block == row_block, blocks_of(block_inverse(diag), 1), 0.0)
    return dot_split(split(final), split(reduced)).astype(BF16)


def part_index():
    return lax.axis_index("section") * 2 + lax.axis_index("sub")


def table_filler(angles_ref, table_ref):
    part = part_index()

    def fill(first):
        rows, sin_rows = slice(first, first + 64), slice(FREQS + first, FREQS + first + 64)
        cos, sin = angles_ref[0, rows, :], angles_ref[1, rows, :]
        step_cos, step_sin = angles_ref[2, rows, :], angles_ref[3, rows, :]
        quarter = ((iota((64, 128), 0) + first) * part) & 3
        odd, minus = (quarter & 1) == 1, quarter >= 2
        cos, sin = jnp.where(odd, -sin, cos), jnp.where(odd, cos, sin)
        cos, sin = jnp.where(minus, -cos, cos), jnp.where(minus, -sin, sin)
        for tile in range(COL_DEV // 128):
            cols = slice(tile * 128, tile * 128 + 128)
            table_ref[rows, cols] = cos.astype(BF16)
            table_ref[sin_rows, cols] = (-sin).astype(BF16)
            cos, sin = cos * step_cos - sin * step_sin, sin * step_cos + cos * step_sin

    steps = [functools.partial(fill, first) for first in range(0, FREQS, 64)]
    return lambda: steps.pop()() if steps else None


def regroup_matrix(inverse):
    out, source = iota((256, 256), 0), iota((256, 256), 1)
    if inverse:
        out, source = source, out
    return hot(source == ((out >> 1) & 7) * 32 + (out >> 4) * 2 + (out & 1)).astype(BF16)


def screen_kernel(
    incidence_hbm,
    coherent_hbm,
    angles_hbm,
    smooth_hbm,
    scale_hbm,
    phases_hbm,
    corrected_ref,
    trend_ref,
    incidence_ref,
    coherent_ref,
    angles_ref,
    smooth_ref,
    scale_ref,
    phases_ref,
    table_ref,
    series_ref,
    residual_ref,
    map_ref,
    pair_out,
    pair_in,
    part_out,
    part_in,
    up_out,
    up_in,
    down_out,
    down_in,
    back_out,
    back_in,
    swap_in,
    flat_ref,
    load_sems,
    send_sems,
    recv_sems,
):
    loads = [
        pltpu.make_async_copy(source, target, load_sems.at[i])
        for i, (source, target) in enumerate(
            [
                (incidence_hbm, incidence_ref),
                (angles_hbm, angles_ref),
                (coherent_hbm, coherent_ref),
                (phases_hbm, phases_ref),
                (smooth_hbm, smooth_ref),
                (scale_hbm, scale_ref),
            ]
        )
    ]
    for load in loads:
        load.start()

    section, grp, sub = (lax.axis_index(name) for name in ("section", "grp", "sub"))
    y, z, x = grp // 64, grp // 4 % 16, grp % 4
    me = sub * 8 + y * 4 + x
    subs, ys = (sub, 1 - sub), (y, 1 - y)
    xs = [(x + hop) % 4 for hop in (2, 1, 3, 0)]
    zs = [(z + hop) % 16 for hop in (8, 7, 9, 6, 10, 5, 11, 4, 12, 3, 13, 2, 14, 1, 15)]
    plane = [
        (b * 8 + c * 4 + d, c * 4 + d, (section, c * 64 + z * 4 + d, b))
        for d in xs
        for b in subs[::-1]
        for c in ys[::-1]
    ][:-1]
    column = [(other, other, (section, y * 64 + other * 4 + x, sub)) for other in zs]
    partner = (1 - section, grp, sub)

    barrier = pltpu.get_barrier_semaphore()
    for device in [partner] + [device for _, _, device in plane + column]:
        pl.semaphore_signal(barrier, inc=1, device_id=device, device_id_type=MESH)

    loads[0].wait()
    loads[1].wait()
    map_ref[...] = pseudo_inverse(incidence_ref[...], table_filler(angles_ref, table_ref))
    epochs = (2.0 * iota((DATES, 1), 0).astype(F32) - (DATES - 1)) / (DATES - 1)
    spread = sum(((2.0 * n - (DATES - 1)) / (DATES - 1)) ** 2 for n in range(DATES))
    for load in loads[2:]:
        load.wait()

    for tile in range(COL_DEV // TILE):
        cols = slice(tile * TILE, tile * TILE + TILE)
        series = dot(map_ref[...], phases_ref[:, cols])
        series_ref[:, cols] = series
        offset = jnp.sum(series, axis=0, keepdims=True) / DATES
        rate = jnp.sum(epochs * series, axis=0, keepdims=True) / spread
        trend_ref[0, :, cols] = offset
        trend_ref[1, :, cols] = rate
        live = coherent_ref[:, cols].astype(F32)
        residual_ref[:, cols] = (live * (series - offset - epochs * rate)).astype(BF16)

    def half_rows(half):
        return pl.ds(pl.multiple_of(half * HALF, HALF), HALF)

    def block(array, number):
        row, col = number // 4 * 32, number % 4 * 128
        return array[row : row + 32, col : col + 128]

    pl.semaphore_wait(barrier, 1 + len(plane) + len(column))

    theirs = dot_nt(residual_ref[half_rows(1 - section), :], table_ref[...]).astype(BF16)
    for number in range(PLANE):
        pair_out[number] = block(theirs, number)
    give = pltpu.make_async_remote_copy(
        src_ref=pair_out,
        dst_ref=pair_in,
        send_sem=send_sems.at[4],
        recv_sem=recv_sems.at[4],
        device_id=partner,
        device_id_type=MESH,
    )
    give.start()
    ours = dot_nt(residual_ref[half_rows(section), :], table_ref[...])
    give.wait_recv()
    for number in range(PLANE):
        part_out[number] = (block(ours, number) + pair_in[number].astype(F32)).astype(BF16)

    def exchange(phase, mine, partners, source, target):
        for other, row, device in partners:
            pltpu.make_async_remote_copy(
                src_ref=source(other, row),
                dst_ref=target.at[mine],
                send_sem=send_sems.at[phase],
                recv_sem=recv_sems.at[phase],
                device_id=device,
                device_id_type=MESH,
            ).start()
        target[mine] = source(mine, lax.rem(mine, SHELF))[...]

    def arrived(phase, target, sems):
        blocks = target.at[pl.ds(0, target.shape[0] - 1)]
        pltpu.make_async_copy(blocks, blocks, sems.at[phase]).wait()

    exchange(0, me, plane, lambda other, row: part_out.at[other], part_in)
    smooth = smooth_ref[...]
    smooth_high = smooth.astype(BF16)
    smooth_low = (smooth - smooth_high.astype(F32)).astype(BF16)
    regroup, ungroup = regroup_matrix(False), regroup_matrix(True)
    arrived(0, part_in, recv_sems)
    row_sum = jnp.sum(part_in[...].astype(F32).reshape(2, 256, 128), axis=0).astype(BF16)
    up_out[...] = dot(regroup, row_sum).astype(BF16).reshape(DEPTH, 16, 128)
    exchange(1, z, column, lambda other, row: up_out.at[other], up_in)
    arrived(1, up_in, recv_sems)
    rows = up_in[...].reshape(256, 128)
    smoothed = dot(smooth_high, rows) + dot(smooth_low, rows)
    down_out[...] = (smoothed * scale_ref[me % 2]).astype(BF16).reshape(DEPTH, 16, 128)
    exchange(2, z, column, lambda other, row: down_out.at[other], down_in)
    arrived(2, down_in, recv_sems)
    whole = down_in[...].reshape(256, 128)
    back_out[...] = dot(ungroup, whole).astype(BF16).reshape(SHELF, 32, 128)
    exchange(3, me, plane, lambda other, row: back_out.at[row], back_in)
    arrived(3, back_in, recv_sems)

    swap = pltpu.make_async_remote_copy(
        src_ref=back_in,
        dst_ref=swap_in,
        send_sem=send_sems.at[5],
        recv_sem=recv_sems.at[5],
        device_id=partner,
        device_id_type=MESH,
    )
    swap.start()

    def correct(half, weights):
        for number in range(PLANE):
            row, col = number // 4 * 32, number % 4 * 128
            flat_ref[row : row + 32, col : col + 128] = weights[number]
        dates = half_rows(half)
        for tile in range(COL_DEV // TILE):
            cols = slice(tile * TILE, tile * TILE + TILE)
            screen = dot(flat_ref[...], table_ref[:, cols]).astype(BF16).astype(F32)
            live = coherent_ref[:, cols].astype(F32)
            corrected_ref[dates, cols] = (live * (series_ref[dates, cols] - screen)).astype(BF16)

    correct(section, back_in)
    give.wait_send()
    arrived(0, part_in, send_sems)
    arrived(1, up_in, send_sems)
    arrived(2, down_in, send_sems)
    arrived(3, back_in, send_sems)
    swap.wait_recv()
    correct(1 - section, swap_in)
    swap.wait_send()


def store_kernel(corrected_ref, trend_ref, corrected_hbm, trend_hbm, sems):
    stores = [
        pltpu.make_async_copy(corrected_ref, corrected_hbm, sems.at[0]),
        pltpu.make_async_copy(trend_ref, trend_hbm, sems.at[1]),
    ]
    for store in stores:
        store.start()
    for store in stores:
        store.wait()


def per_device(phases, incidence, coherent):
    ifgs = phases.shape[0]
    in_hbm = pl.BlockSpec(memory_space=pltpu.HBM)
    in_vmem = pl.BlockSpec(memory_space=pltpu.VMEM)
    results = (
        jax.ShapeDtypeStruct((DATES, COL_DEV), BF16),
        jax.ShapeDtypeStruct((2, 1, COL_DEV), F32),
    )
    operands = (
        incidence.T,
        coherent,
        jnp.asarray(angle_tables()),
        jnp.asarray(smoothing_matrix()),
        jnp.asarray(column_scales()),
        phases.reshape(ifgs, COL_DEV),
    )
    corrected, trend_fit = pl.pallas_call(
        screen_kernel,
        out_shape=results,
        in_specs=[in_hbm] * 6,
        out_specs=(in_vmem, in_vmem),
        scratch_shapes=[
            pltpu.VMEM((2, ifgs), jnp.int32),
            pltpu.VMEM((1, COL_DEV), jnp.int32),
            pltpu.VMEM((4, FREQS, 128), F32),
            pltpu.VMEM((256, 256), F32),
            pltpu.VMEM((2, 1, 128), F32),
            pltpu.VMEM((ifgs, COL_DEV), BF16),
            pltpu.VMEM((2 * FREQS, COL_DEV), BF16),
            pltpu.VMEM((DATES, COL_DEV), F32),
            pltpu.VMEM((DATES, COL_DEV), BF16),
            pltpu.VMEM((DATES, ifgs), BF16),
            pltpu.VMEM((PLANE, 32, 128), BF16),
            pltpu.VMEM((PLANE, 32, 128), BF16),
            pltpu.VMEM((PLANE, 32, 128), BF16),
            pltpu.VMEM((PLANE, 32, 128), BF16),
            pltpu.VMEM((DEPTH, 16, 128), BF16),
            pltpu.VMEM((DEPTH, 16, 128), BF16),
            pltpu.VMEM((DEPTH, 16, 128), BF16),
            pltpu.VMEM((DEPTH, 16, 128), BF16),
            pltpu.VMEM((SHELF, 32, 128), BF16),
            pltpu.VMEM((PLANE, 32, 128), BF16),
            pltpu.VMEM((PLANE, 32, 128), BF16),
            pltpu.VMEM((HALF, 2 * FREQS), BF16),
            pltpu.SemaphoreType.DMA((6,)),
            pltpu.SemaphoreType.DMA((6,)),
            pltpu.SemaphoreType.DMA((6,)),
        ],
        compiler_params=pltpu.CompilerParams(
            collective_id=0, has_side_effects=True, vmem_limit_bytes=36 * 2**20
        ),
        name="screen",
    )(*(pltpu.with_memory_space_constraint(operand, pltpu.HBM) for operand in operands))
    corrected, trend_fit = pl.pallas_call(
        store_kernel,
        out_shape=results,
        in_specs=[in_vmem] * 2,
        out_specs=(in_hbm, in_hbm),
        scratch_shapes=[pltpu.SemaphoreType.DMA((2,))],
        compiler_params=pltpu.CompilerParams(vmem_limit_bytes=8 * 2**20),
        name="store",
    )(corrected, trend_fit)
    return (corrected.reshape(DATES, 1, COL_DEV), trend_fit)


def solution(mesh):
    placed = (P(None, "grp", ("section", "sub")), P(), P("grp", ("section", "sub")))
    return jax.shard_map(
        per_device,
        mesh=mesh,
        in_specs=placed,
        out_specs=(P(None, "grp", ("section", "sub")), P(None, "grp", ("section", "sub"))),
        check_vma=False,
    )
```

```python
import functools
import math

import jax
import jax.numpy as jnp
import numpy as np
from jax import lax
from jax.experimental import pallas as pl
from jax.experimental.pallas import tpu as pltpu
from jax.sharding import PartitionSpec as P

MESH = pl.DeviceIdType.MESH
F32 = jnp.float32
BF16 = jnp.bfloat16

REG = 0.1
FREQS = 256
DATES = 256
ROWS = 128
COLS = 8192
BLOCKS = DATES // 8
COL_DEV = 2048
TILE = 512

PLANE = 16
HALF = DATES // 2
DEPTH = 16
SHELF = 8


def angle_tables():
    frequency = np.arange(FREQS, dtype=np.int64)[:, None]
    column = np.arange(128, dtype=np.int64)[None, :]
    start = (frequency * column % COLS) * (2.0 * math.pi / COLS)
    step = (frequency * np.full_like(column, 128) % COLS) * (2.0 * math.pi / COLS)
    return np.stack([np.cos(start), np.sin(start), np.cos(step), np.sin(step)]).astype(np.float32)


def row_filter():
    indices = np.arange(ROWS)
    frequency = np.minimum(indices, ROWS - indices).astype(np.float64)
    taper = np.exp(-np.square(frequency / (ROWS / 4.0)))
    turns = (indices[:, None] * indices[None, :] % ROWS) * (2.0 * math.pi / ROWS)
    cos_rows, sin_rows = np.cos(turns), np.sin(turns)
    return ((cos_rows * taper) @ cos_rows.T + (sin_rows * taper) @ sin_rows.T) / ROWS


def smoothing_matrix():
    index = np.arange(DEPTH * SHELF * 2)
    z, shelf, half = index // 16, index // 2 % 8, index % 2
    row = shelf // 4 * 64 + z * 4 + shelf % 4
    full = row_filter()[row[:, None], row[None, :]] * (half[:, None] == half[None, :])
    return full.astype(np.float32)


def column_scales():
    frequency = np.arange(FREQS)
    scale = np.where(frequency == 0, 1.0, 2.0) * np.exp(-np.square(frequency / FREQS)) / COLS
    return scale.astype(np.float32).reshape(2, 1, 128)


def iota(shape, axis):
    return lax.broadcasted_iota(jnp.int32, shape, axis)


def hot(condition):
    return jnp.where(condition, 1.0, 0.0).astype(F32)


def dot(a, b):
    return jnp.dot(a, b, preferred_element_type=F32)


def dot_nt(a, b):
    return lax.dot_general(a, b, (((1,), (1,)), ((), ())), preferred_element_type=F32)


def lane_roll(x, shift):
    flat = x.reshape(64, 128)
    return pltpu.roll(flat, shift, 1).reshape(8, 8, 128)


def block_product(a, b):
    terms = [a[:, k : k + 1, :] * b[k][None] for k in range(8)]
    while len(terms) > 1:
        terms = [one + two for one, two in zip(terms[::2], terms[1::2])]
    return terms[0]


def reciprocal(x):
    guess = pl.reciprocal(x, approx=True)
    guess = guess * (2.0 - x * guess)
    return guess * (2.0 - x * guess)


def block_inverse(d):
    sub = iota((8, 128), 0)
    rows = [d[i] for i in range(8)]
    for k in range(0, 8, 2):
        a, b = rows[k][k : k + 1, :], rows[k][k + 1 : k + 2, :]
        c, e = rows[k + 1][k : k + 1, :], rows[k + 1][k + 1 : k + 2, :]
        scale = reciprocal(a * e - b * c)
        one, two = sub == k, sub == k + 1
        first = jnp.where(one, 1.0, jnp.where(two, 0.0, rows[k]))
        second = jnp.where(one, 0.0, jnp.where(two, 1.0, rows[k + 1]))
        top = (e * scale) * first - (b * scale) * second
        bottom = (a * scale) * second - (c * scale) * first
        for i in range(8):
            if i not in (k, k + 1):
                f, g = rows[i][k : k + 1, :], rows[i][k + 1 : k + 2, :]
                rest = jnp.where(one | two, 0.0, rows[i])
                rows[i] = rest - (f * top + g * bottom)
        rows[k], rows[k + 1] = top, bottom
    return jnp.stack(rows)


def split(x):
    high = x.astype(BF16)
    rest = x - high.astype(F32)
    middle = rest.astype(BF16)
    return high, middle, (rest - middle.astype(F32)).astype(BF16)


def dot_split(a, b):
    (ah, am, al), (bh, bm, bl) = a, b
    return dot(
        jnp.concatenate([al, am, ah, am, ah, ah], axis=1),
        jnp.concatenate([bh, bm, bl, bh, bm, bh], axis=0),
    )


def pseudo_inverse(incidence, beside):
    count = incidence.shape[1]
    primary, secondary = incidence[0:1, :], incidence[1:2, :]
    dates = iota((DATES, count), 0)
    design_t = hot(dates == secondary) - hot(dates == primary)
    p_in, p_block, s_in, s_block = primary & 7, primary >> 3, secondary & 7, secondary >> 3
    block = iota((128, count), 0) & (BLOCKS - 1)
    at_primary = hot(block == p_block).astype(BF16)
    at_secondary = hot(block == s_block).astype(BF16)
    pair = iota((64, count), 0)
    same = hot(p_block == s_block)
    ps = hot(pair == p_in * 8 + s_in)
    sp = hot(pair == s_in * 8 + p_in)
    on_primary = hot(pair == p_in * 9) - same * (ps + sp)
    on_secondary = hot(pair == s_in * 9)
    to_next = (same - 1.0) * ps
    to_last = (same - 1.0) * sp
    from_primary = dot_nt(jnp.concatenate([on_primary, to_next], 0).astype(BF16), at_primary)
    from_secondary = dot_nt(jnp.concatenate([on_secondary, to_last], 0).astype(BF16), at_secondary)
    entry = iota((64, 128), 0)
    eye = hot((entry >> 3) == (entry & 7))
    diag = (from_primary[:64] + from_secondary[:64] + REG * eye).reshape(8, 8, 128)
    below = from_secondary[64:].reshape(8, 8, 128)
    above = from_primary[64:].reshape(8, 8, 128)
    first = (iota((8, 8, 128), 2) & BLOCKS) == 0

    date = iota((2 * DATES, 128), 0)
    take = hot((date >> 3) == iota((2 * DATES, 128), 1)).astype(BF16)
    own_row = ((iota((2 * DATES, 192), 1) >> 3) & 7) == (iota((2 * DATES, 192), 0) & 7)
    spread = hot((iota((192, DATES), 1) & 7) == (iota((192, DATES), 0) & 7)).astype(BF16)
    row_block = iota((DATES, DATES), 0) >> 3
    col_block = iota((DATES, DATES), 1) >> 3

    def blocks_of(x, sides):
        count = sides * DATES
        terms = jnp.concatenate(split(x.reshape(64, 128)), axis=0)
        rows = jnp.where(own_row[:count], dot_nt(take[:count], terms), 0.0).astype(BF16)
        return dot(rows, spread)

    total = None
    step = 1
    while step < BLOCKS:
        beside()
        inverse = block_inverse(diag)
        near = jnp.where(first, lane_roll(inverse, step), lane_roll(inverse, 128 - step))
        gain = block_product(jnp.where(first, below, above), near)
        back = jnp.where(first, lane_roll(above, step), lane_roll(below, 128 - step))
        change = block_product(gain, back)
        diag = diag - change - lane_roll(change, BLOCKS)
        sides = blocks_of(gain, 2)
        gamma = jnp.where(
            col_block == row_block - step,
            sides[:DATES],
            jnp.where(col_block == row_block + step, sides[DATES:], 0.0),
        )
        if total is None:
            total = hot(iota((DATES, DATES), 0) == iota((DATES, DATES), 1)) - gamma
        else:
            total = total - dot_split(split(gamma), split(total))
        if 2 * step < BLOCKS:
            far = jnp.where(first, lane_roll(below, step), lane_roll(above, 128 - step))
            links = -block_product(gain, far)
            swapped = lane_roll(links, BLOCKS)
            below = jnp.where(first, links, swapped)
            above = jnp.where(first, swapped, links)
        step *= 2
    design_t = design_t.astype(BF16)
    reduced = dot(
        jnp.concatenate(split(total)[::-1], axis=1),
        jnp.concatenate([design_t, design_t, design_t], axis=0),
    )
    final = jnp.where(col_block == row_block, blocks_of(block_inverse(diag), 1), 0.0)
    return dot_split(split(final), split(reduced)).astype(BF16)


def part_index():
    return lax.axis_index("section") * 2 + lax.axis_index("sub")


def table_filler(angles_ref, table_ref):
    part = part_index()

    def fill(first):
        rows, sin_rows = slice(first, first + 64), slice(FREQS + first, FREQS + first + 64)
        cos, sin = angles_ref[0, rows, :], angles_ref[1, rows, :]
        step_cos, step_sin = angles_ref[2, rows, :], angles_ref[3, rows, :]
        quarter = ((iota((64, 128), 0) + first) * part) & 3
        odd, minus = (quarter & 1) == 1, quarter >= 2
        cos, sin = jnp.where(odd, -sin, cos), jnp.where(odd, cos, sin)
        cos, sin = jnp.where(minus, -cos, cos), jnp.where(minus, -sin, sin)
        for tile in range(COL_DEV // 128):
            cols = slice(tile * 128, tile * 128 + 128)
            table_ref[rows, cols] = cos.astype(BF16)
            table_ref[sin_rows, cols] = (-sin).astype(BF16)
            cos, sin = cos * step_cos - sin * step_sin, sin * step_cos + cos * step_sin

    steps = [functools.partial(fill, first) for first in range(0, FREQS, 64)]
    return lambda: steps.pop()() if steps else None


def regroup_matrix():
    out, source = iota((128, 128), 0), iota((128, 128), 1)
    return hot(source == ((out >> 1) & 7) * 16 + (out >> 4) * 2 + (out & 1)).astype(BF16)


def screen_kernel(
    incidence_hbm,
    coherent_hbm,
    angles_hbm,
    smooth_hbm,
    scale_hbm,
    phases_hbm,
    corrected_ref,
    trend_ref,
    incidence_ref,
    coherent_ref,
    angles_ref,
    smooth_ref,
    scale_ref,
    phases_ref,
    table_ref,
    series_ref,
    residual_ref,
    map_ref,
    pair_out,
    pair_in,
    part_out,
    part_in,
    up_out,
    up_in,
    down_out,
    down_in,
    back_out,
    back_in,
    swap_in,
    flat_ref,
    load_sems,
    send_sems,
    recv_sems,
):
    loads = [
        pltpu.make_async_copy(source, target, load_sems.at[i])
        for i, (source, target) in enumerate(
            [
                (incidence_hbm, incidence_ref),
                (angles_hbm, angles_ref),
                (coherent_hbm, coherent_ref),
                (phases_hbm, phases_ref),
                (smooth_hbm, smooth_ref),
                (scale_hbm, scale_ref),
            ]
        )
    ]
    for load in loads:
        load.start()

    section, grp, sub = (lax.axis_index(name) for name in ("section", "grp", "sub"))
    y, z, x = grp // 64, grp // 4 % 16, grp % 4
    me = sub * 8 + y * 4 + x
    subs, ys = (sub, 1 - sub), (y, 1 - y)
    xs = [(x + hop) % 4 for hop in (2, 1, 3, 0)]
    plane = [
        (b * 8 + c * 4 + d, c * 4 + d, (section, c * 64 + z * 4 + d, b))
        for d in xs
        for b in subs[::-1]
        for c in ys[::-1]
    ][:-1]
    own, away = z % 2, 1 - z % 2
    pairs = [(z // 2 + hop) % 8 for hop in (4, 3, 5, 2, 6, 1, 7, 0)]

    def column(pair, parity):
        other = pair * 2 + parity
        return other, (section, y * 64 + other * 4 + x, sub)

    lines = [
        [(pair, *column(pair, away)) for pair in pairs],
        [(pair, *column(pair, own)) for pair in pairs[:-1]],
    ]
    partner = (1 - section, grp, sub)

    barrier = pltpu.get_barrier_semaphore()
    peers = [partner] + [device for _, _, device in plane + lines[0] + lines[1]]
    for device in peers:
        pl.semaphore_signal(barrier, inc=1, device_id=device, device_id_type=MESH)

    loads[0].wait()
    loads[1].wait()
    map_ref[...] = pseudo_inverse(incidence_ref[...], table_filler(angles_ref, table_ref))
    epochs = (2.0 * iota((DATES, 1), 0).astype(F32) - (DATES - 1)) / (DATES - 1)
    spread = sum(((2.0 * n - (DATES - 1)) / (DATES - 1)) ** 2 for n in range(DATES))
    for load in loads[2:]:
        load.wait()

    for tile in range(COL_DEV // TILE):
        cols = slice(tile * TILE, tile * TILE + TILE)
        series = dot(map_ref[...], phases_ref[:, cols])
        series_ref[:, cols] = series
        offset = jnp.sum(series, axis=0, keepdims=True) / DATES
        rate = jnp.sum(epochs * series, axis=0, keepdims=True) / spread
        trend_ref[0, :, cols] = offset
        trend_ref[1, :, cols] = rate
        live = coherent_ref[:, cols].astype(F32)
        residual_ref[:, cols] = (live * (series - offset - epochs * rate)).astype(BF16)

    def half_rows(half):
        return pl.ds(pl.multiple_of(half * HALF, HALF), HALF)

    def block(array, number):
        row, col = number // 4 * 32, number % 4 * 128
        return array[row : row + 32, col : col + 128]

    pl.semaphore_wait(barrier, len(peers))

    theirs = dot_nt(residual_ref[half_rows(1 - section), :], table_ref[...]).astype(BF16)
    for number in range(PLANE):
        pair_out[number] = block(theirs, number)
    def copy(number, source, target, device):
        return pltpu.make_async_remote_copy(
            src_ref=source,
            dst_ref=target,
            send_sem=send_sems.at[number],
            recv_sem=recv_sems.at[number],
            device_id=device,
            device_id_type=MESH,
        )

    def wait(sems, number, blocks):
        pltpu.make_async_copy(blocks, blocks, sems.at[number]).wait()

    some = [up_in.at[pl.ds(0, len(line))] for line in lines]
    most = back_in.at[0, pl.ds(0, len(plane))]

    give = copy(10, pair_out, pair_in, partner)
    give.start()
    ours = dot_nt(residual_ref[half_rows(section), :], table_ref[...])
    give.wait_recv()
    for number in range(PLANE):
        both = (block(ours, number) + pair_in[number].astype(F32)).astype(BF16)
        part_out[0, number] = both[:16]
        part_out[1, number] = both[16:]

    for turn, parity in enumerate((away, own)):
        for other, _, device in plane:
            copy(turn, part_out.at[parity, other], part_in.at[parity, me], device).start()
        part_in[parity, me] = part_out[parity, me]

    smooth = smooth_ref[...]
    smooth_high = smooth.astype(BF16)
    smooth_low = (smooth - smooth_high.astype(F32)).astype(BF16)
    regroup = regroup_matrix()

    for turn, parity in enumerate((away, own)):
        wait(recv_sems, turn, most)
        row_sum = jnp.sum(part_in[parity].astype(F32).reshape(2, 128, 128), axis=0).astype(BF16)
        up_out[parity] = dot(regroup, row_sum).astype(BF16).reshape(8, 16, 128)
        for pair, _, device in lines[turn]:
            copy(2 + turn, up_out.at[parity, pair], up_in.at[z], device).start()
    up_in[z] = up_out[own, z // 2]

    wait(recv_sems, 2, some[0])
    wait(recv_sems, 3, some[1])
    rows = up_in[...].reshape(256, 128)
    smoothed = dot(smooth_high, rows) + dot(smooth_low, rows)
    down_out[...] = (smoothed * scale_ref[me % 2]).astype(BF16).reshape(DEPTH, 16, 128)
    for turn in range(2):
        for _, other, device in lines[turn]:
            copy(4 + turn, down_out.at[other], down_in.at[own, z // 2], device).start()
    down_in[own, z // 2] = down_out[z]

    for turn, parity in enumerate((away, own)):
        wait(recv_sems, 4 + turn, some[turn])
        whole = down_in[parity].reshape(128, 128)
        back_out[parity] = dot(regroup, whole).astype(BF16).reshape(SHELF, 16, 128)
        for _, row, device in plane:
            copy(6 + turn, back_out.at[parity, row], back_in.at[parity, me], device).start()
        back_in[parity, me] = back_out[parity, lax.rem(me, SHELF)]

    swaps = [
        copy(8 + turn, back_in.at[parity], swap_in.at[parity], partner)
        for turn, parity in enumerate((away, own))
    ]
    for turn, swap in enumerate(swaps):
        wait(recv_sems, 6 + turn, most)
        swap.start()

    def correct(half, weights):
        for number in range(PLANE):
            row, col = number // 4 * 32, number % 4 * 128
            flat_ref[row : row + 16, col : col + 128] = weights[0, number]
            flat_ref[row + 16 : row + 32, col : col + 128] = weights[1, number]
        dates = half_rows(half)
        for tile in range(COL_DEV // TILE):
            cols = slice(tile * TILE, tile * TILE + TILE)
            screen = dot(flat_ref[...], table_ref[:, cols]).astype(BF16).astype(F32)
            live = coherent_ref[:, cols].astype(F32)
            corrected_ref[dates, cols] = (live * (series_ref[dates, cols] - screen)).astype(BF16)

    correct(section, back_in)
    give.wait_send()
    for turn in range(2):
        wait(send_sems, turn, most)
        wait(send_sems, 2 + turn, some[turn])
        wait(send_sems, 4 + turn, some[turn])
        wait(send_sems, 6 + turn, most)
    for swap in swaps:
        swap.wait_recv()
    correct(1 - section, swap_in)
    for swap in swaps:
        swap.wait_send()


def store_kernel(corrected_ref, trend_ref, corrected_hbm, trend_hbm, sems):
    stores = [
        pltpu.make_async_copy(corrected_ref, corrected_hbm, sems.at[0]),
        pltpu.make_async_copy(trend_ref, trend_hbm, sems.at[1]),
    ]
    for store in stores:
        store.start()
    for store in stores:
        store.wait()


def per_device(phases, incidence, coherent):
    ifgs = phases.shape[0]
    in_hbm = pl.BlockSpec(memory_space=pltpu.HBM)
    in_vmem = pl.BlockSpec(memory_space=pltpu.VMEM)
    results = (
        jax.ShapeDtypeStruct((DATES, COL_DEV), BF16),
        jax.ShapeDtypeStruct((2, 1, COL_DEV), F32),
    )
    operands = (
        incidence.T,
        coherent,
        jnp.asarray(angle_tables()),
        jnp.asarray(smoothing_matrix()),
        jnp.asarray(column_scales()),
        phases.reshape(ifgs, COL_DEV),
    )
    corrected, trend_fit = pl.pallas_call(
        screen_kernel,
        out_shape=results,
        in_specs=[in_hbm] * 6,
        out_specs=(in_vmem, in_vmem),
        scratch_shapes=[
            pltpu.VMEM((2, ifgs), jnp.int32),
            pltpu.VMEM((1, COL_DEV), jnp.int32),
            pltpu.VMEM((4, FREQS, 128), F32),
            pltpu.VMEM((256, 256), F32),
            pltpu.VMEM((2, 1, 128), F32),
            pltpu.VMEM((ifgs, COL_DEV), BF16),
            pltpu.VMEM((2 * FREQS, COL_DEV), BF16),
            pltpu.VMEM((DATES, COL_DEV), F32),
            pltpu.VMEM((DATES, COL_DEV), BF16),
            pltpu.VMEM((DATES, ifgs), BF16),
            pltpu.VMEM((PLANE, 32, 128), BF16),
            pltpu.VMEM((PLANE, 32, 128), BF16),
            pltpu.VMEM((2, PLANE, 16, 128), BF16),
            pltpu.VMEM((2, PLANE, 16, 128), BF16),
            pltpu.VMEM((2, 8, 16, 128), BF16),
            pltpu.VMEM((DEPTH, 16, 128), BF16),
            pltpu.VMEM((DEPTH, 16, 128), BF16),
            pltpu.VMEM((2, 8, 16, 128), BF16),
            pltpu.VMEM((2, SHELF, 16, 128), BF16),
            pltpu.VMEM((2, PLANE, 16, 128), BF16),
            pltpu.VMEM((2, PLANE, 16, 128), BF16),
            pltpu.VMEM((HALF, 2 * FREQS), BF16),
            pltpu.SemaphoreType.DMA((6,)),
            pltpu.SemaphoreType.DMA((11,)),
            pltpu.SemaphoreType.DMA((11,)),
        ],
        compiler_params=pltpu.CompilerParams(
            collective_id=0, has_side_effects=True, vmem_limit_bytes=36 * 2**20
        ),
        name="screen",
    )(*(pltpu.with_memory_space_constraint(operand, pltpu.HBM) for operand in operands))
    corrected, trend_fit = pl.pallas_call(
        store_kernel,
        out_shape=results,
        in_specs=[in_vmem] * 2,
        out_specs=(in_hbm, in_hbm),
        scratch_shapes=[pltpu.SemaphoreType.DMA((2,))],
        compiler_params=pltpu.CompilerParams(vmem_limit_bytes=8 * 2**20),
        name="store",
    )(corrected, trend_fit)
    return (corrected.reshape(DATES, 1, COL_DEV), trend_fit)


def solution(mesh):
    placed = (P(None, "grp", ("section", "sub")), P(), P("grp", ("section", "sub")))
    return jax.shard_map(
        per_device,
        mesh=mesh,
        in_specs=placed,
        out_specs=(P(None, "grp", ("section", "sub")), P(None, "grp", ("section", "sub"))),
        check_vma=False,
    )
```

```python
import math

import jax
import jax.numpy as jnp
import numpy as np
from jax import lax
from jax.experimental import pallas as pl
from jax.experimental.pallas import tpu as pltpu
from jax.sharding import PartitionSpec as P

MESH = pl.DeviceIdType.MESH
F32 = jnp.float32
BF16 = jnp.bfloat16

REG = 0.1
FREQS = 256
DATES = 256
ROWS = 128
COLS = 8192
BLOCKS = DATES // 8
COL_DEV = 2048
TILE = 512

PLANE = 16
HALF = DATES // 2
DEPTH = 16
SHELF = 8


def angle_tables():
    frequency = np.arange(FREQS, dtype=np.int64)[:, None]
    column = np.arange(128, dtype=np.int64)[None, :]
    start = (frequency * column % COLS) * (2.0 * math.pi / COLS)
    step = (frequency * np.full_like(column, 128) % COLS) * (2.0 * math.pi / COLS)
    return np.stack([np.cos(start), np.sin(start), np.cos(step), np.sin(step)]).astype(np.float32)


def row_filter():
    indices = np.arange(ROWS)
    frequency = np.minimum(indices, ROWS - indices).astype(np.float64)
    taper = np.exp(-np.square(frequency / (ROWS / 4.0)))
    turns = (indices[:, None] * indices[None, :] % ROWS) * (2.0 * math.pi / ROWS)
    cos_rows, sin_rows = np.cos(turns), np.sin(turns)
    return ((cos_rows * taper) @ cos_rows.T + (sin_rows * taper) @ sin_rows.T) / ROWS


def smoothing_matrix():
    index = np.arange(DEPTH * SHELF * 2)
    z, shelf, half = index // 16, index // 2 % 8, index % 2
    row = shelf // 4 * 64 + z * 4 + shelf % 4
    full = row_filter()[row[:, None], row[None, :]] * (half[:, None] == half[None, :])
    return full.astype(np.float32)


def column_scales():
    frequency = np.arange(FREQS)
    scale = np.where(frequency == 0, 1.0, 2.0) * np.exp(-np.square(frequency / FREQS)) / COLS
    return scale.astype(np.float32).reshape(2, 1, 128)


def iota(shape, axis):
    return lax.broadcasted_iota(jnp.int32, shape, axis)


def hot(condition):
    return jnp.where(condition, 1.0, 0.0).astype(F32)


def dot(a, b):
    return jnp.dot(a, b, preferred_element_type=F32)


def dot_nt(a, b):
    return lax.dot_general(a, b, (((1,), (1,)), ((), ())), preferred_element_type=F32)


def lane_roll(x, shift):
    flat = x.reshape(64, 128)
    return pltpu.roll(flat, shift, 1).reshape(8, 8, 128)


def block_product(a, b):
    terms = [a[:, k : k + 1, :] * b[k][None] for k in range(8)]
    while len(terms) > 1:
        terms = [one + two for one, two in zip(terms[::2], terms[1::2])]
    return terms[0]


def reciprocal(x):
    guess = pl.reciprocal(x, approx=True)
    guess = guess * (2.0 - x * guess)
    return guess * (2.0 - x * guess)


def block_inverse(d):
    sub = iota((8, 128), 0)
    rows = [d[i] for i in range(8)]
    for k in range(0, 8, 2):
        a, b = rows[k][k : k + 1, :], rows[k][k + 1 : k + 2, :]
        c, e = rows[k + 1][k : k + 1, :], rows[k + 1][k + 1 : k + 2, :]
        scale = reciprocal(a * e - b * c)
        one, two = sub == k, sub == k + 1
        first = jnp.where(one, 1.0, jnp.where(two, 0.0, rows[k]))
        second = jnp.where(one, 0.0, jnp.where(two, 1.0, rows[k + 1]))
        top = (e * scale) * first - (b * scale) * second
        bottom = (a * scale) * second - (c * scale) * first
        for i in range(8):
            if i not in (k, k + 1):
                f, g = rows[i][k : k + 1, :], rows[i][k + 1 : k + 2, :]
                rest = jnp.where(one | two, 0.0, rows[i])
                rows[i] = rest - (f * top + g * bottom)
        rows[k], rows[k + 1] = top, bottom
    return jnp.stack(rows)


def split(x):
    high = x.astype(BF16)
    rest = x - high.astype(F32)
    middle = rest.astype(BF16)
    return high, middle, (rest - middle.astype(F32)).astype(BF16)


def dot_split(a, b):
    (ah, am, al), (bh, bm, bl) = a, b
    return dot(
        jnp.concatenate([al, am, ah, am, ah, ah], axis=1),
        jnp.concatenate([bh, bm, bl, bh, bm, bh], axis=0),
    )


def pseudo_inverse(incidence, total_ref):
    count = incidence.shape[1]
    primary, secondary = incidence[0:1, :], incidence[1:2, :]
    dates = iota((DATES, count), 0)
    design_t = hot(dates == secondary) - hot(dates == primary)
    p_in, p_block, s_in, s_block = primary & 7, primary >> 3, secondary & 7, secondary >> 3
    block = iota((128, count), 0) & (BLOCKS - 1)
    at_primary = hot(block == p_block).astype(BF16)
    at_secondary = hot(block == s_block).astype(BF16)
    pair = iota((64, count), 0)
    same = hot(p_block == s_block)
    ps = hot(pair == p_in * 8 + s_in)
    sp = hot(pair == s_in * 8 + p_in)
    on_primary = hot(pair == p_in * 9) - same * (ps + sp)
    on_secondary = hot(pair == s_in * 9)
    to_next = (same - 1.0) * ps
    to_last = (same - 1.0) * sp
    from_primary = dot_nt(jnp.concatenate([on_primary, to_next], 0).astype(BF16), at_primary)
    from_secondary = dot_nt(jnp.concatenate([on_secondary, to_last], 0).astype(BF16), at_secondary)
    entry = iota((64, 128), 0)
    eye = hot((entry >> 3) == (entry & 7))
    diag = (from_primary[:64] + from_secondary[:64] + REG * eye).reshape(8, 8, 128)
    below = from_secondary[64:].reshape(8, 8, 128)
    above = from_primary[64:].reshape(8, 8, 128)
    first = (iota((8, 8, 128), 2) & BLOCKS) == 0

    date = iota((2 * DATES, 128), 0)
    take = hot((date >> 3) == iota((2 * DATES, 128), 1)).astype(BF16)
    own_row = ((iota((2 * DATES, 192), 1) >> 3) & 7) == (iota((2 * DATES, 192), 0) & 7)
    spread = hot((iota((192, DATES), 1) & 7) == (iota((192, DATES), 0) & 7)).astype(BF16)
    row_block = iota((DATES, DATES), 0) >> 3
    col_block = iota((DATES, DATES), 1) >> 3

    def blocks_of(x, sides):
        count = sides * DATES
        terms = jnp.concatenate(split(x.reshape(64, 128)), axis=0)
        rows = jnp.where(own_row[:count], dot_nt(take[:count], terms), 0.0).astype(BF16)
        return dot(rows, spread)

    def apply(gain, step):
        sides = blocks_of(gain, 2)
        gamma = jnp.where(
            col_block == row_block - step,
            sides[:DATES],
            jnp.where(col_block == row_block + step, sides[DATES:], 0.0),
        )
        total = total_ref[...]
        total_ref[...] = total - dot_split(split(gamma), split(total))

    def level(_, carry):
        step, last_step, diag, below, above, last_gain = carry
        apply(last_gain, last_step)
        inverse = block_inverse(diag)
        near = jnp.where(first, lane_roll(inverse, step), lane_roll(inverse, 128 - step))
        gain = block_product(jnp.where(first, below, above), near)
        back = jnp.where(first, lane_roll(above, step), lane_roll(below, 128 - step))
        change = block_product(gain, back)
        diag = diag - change - lane_roll(change, BLOCKS)
        far = jnp.where(first, lane_roll(below, step), lane_roll(above, 128 - step))
        links = -block_product(gain, far)
        swapped = lane_roll(links, BLOCKS)
        below = jnp.where(first, links, swapped)
        above = jnp.where(first, swapped, links)
        return step * 2, step, diag, below, above, gain

    total_ref[...] = hot(iota((DATES, DATES), 0) == iota((DATES, DATES), 1))
    start = (jnp.int32(1), jnp.int32(0), diag, below, above, jnp.zeros((8, 8, 128), F32))
    levels = BLOCKS.bit_length() - 1
    _, last_step, diag, _, _, last_gain = lax.fori_loop(0, levels, level, start)
    apply(last_gain, last_step)
    total = total_ref[...]
    design_t = design_t.astype(BF16)
    reduced = dot(
        jnp.concatenate(split(total)[::-1], axis=1),
        jnp.concatenate([design_t, design_t, design_t], axis=0),
    )
    final = jnp.where(col_block == row_block, blocks_of(block_inverse(diag), 1), 0.0)
    return dot_split(split(final), split(reduced)).astype(BF16)


def part_index():
    return lax.axis_index("section") * 2 + lax.axis_index("sub")


def fill_table(angles_ref, table_ref):
    @pl.loop(0, FREQS // 64)
    def _(group):
        first = pl.multiple_of(group * 64, 64)
        rows, sin_rows = pl.ds(first, 64), pl.ds(first + FREQS, 64)
        cos, sin = angles_ref[0, rows, :], angles_ref[1, rows, :]
        step_cos, step_sin = angles_ref[2, rows, :], angles_ref[3, rows, :]
        quarter = ((iota((64, 128), 0) + first) * part_index()) & 3
        odd, minus = (quarter & 1) == 1, quarter >= 2
        cos, sin = jnp.where(odd, -sin, cos), jnp.where(odd, cos, sin)
        cos, sin = jnp.where(minus, -cos, cos), jnp.where(minus, -sin, sin)
        for tile in range(COL_DEV // 128):
            cols = slice(tile * 128, tile * 128 + 128)
            table_ref[rows, cols] = cos.astype(BF16)
            table_ref[sin_rows, cols] = (-sin).astype(BF16)
            cos, sin = cos * step_cos - sin * step_sin, sin * step_cos + cos * step_sin


def regroup_matrix(inverse):
    out, source = iota((256, 256), 0), iota((256, 256), 1)
    if inverse:
        out, source = source, out
    return hot(source == ((out >> 1) & 7) * 32 + (out >> 4) * 2 + (out & 1)).astype(BF16)


def screen_kernel(
    incidence_hbm,
    coherent_hbm,
    angles_hbm,
    smooth_hbm,
    scale_hbm,
    phases_hbm,
    corrected_ref,
    trend_ref,
    incidence_ref,
    coherent_ref,
    angles_ref,
    smooth_ref,
    scale_ref,
    phases_ref,
    table_ref,
    series_ref,
    spectrum_ref,
    map_ref,
    total_ref,
    pair_out,
    pair_in,
    part_out,
    part_in,
    up_out,
    up_in,
    down_out,
    down_in,
    back_out,
    back_in,
    swap_in,
    flat_ref,
    load_sems,
    send_sems,
    recv_sems,
):
    loads = [
        pltpu.make_async_copy(source, target, load_sems.at[i])
        for i, (source, target) in enumerate(
            [
                (incidence_hbm, incidence_ref),
                (angles_hbm, angles_ref),
                (coherent_hbm, coherent_ref),
                (phases_hbm, phases_ref),
                (smooth_hbm, smooth_ref),
                (scale_hbm, scale_ref),
            ]
        )
    ]
    for load in loads:
        load.start()

    section, grp, sub = (lax.axis_index(name) for name in ("section", "grp", "sub"))
    y, z, x = grp // 64, grp // 4 % 16, grp % 4
    me = sub * 8 + y * 4 + x
    def in_plane(hop):
        other = lax.rem(me + hop, PLANE)
        row = lax.rem(other, SHELF)
        x_other = lax.rem(other, 4)
        grp_other = lax.div(row, 4) * 64 + z * 4 + x_other
        return other, row, (section, grp_other, lax.div(other, SHELF))

    def along_z(hop):
        other = lax.rem(z + hop, DEPTH)
        return other, other, (section, grp + (other - z) * 4, sub)

    partner = (1 - section, grp, sub)

    barrier = pltpu.get_barrier_semaphore()
    pl.semaphore_signal(barrier, inc=1, device_id=partner, device_id_type=MESH)

    @pl.loop(1, PLANE)
    def _(hop):
        for near in (in_plane, along_z):
            pl.semaphore_signal(barrier, inc=1, device_id=near(hop)[2], device_id_type=MESH)

    loads[1].wait()
    fill_table(angles_ref, table_ref)
    loads[0].wait()
    map_ref[...] = pseudo_inverse(incidence_ref[...], total_ref)
    spectrum_ref[...] = jnp.zeros_like(spectrum_ref)
    epochs = (2.0 * iota((DATES, 1), 0).astype(F32) - (DATES - 1)) / (DATES - 1)
    spread = sum(((2.0 * n - (DATES - 1)) / (DATES - 1)) ** 2 for n in range(DATES))
    for load in loads[2:]:
        load.wait()

    @pl.loop(0, COL_DEV // TILE)
    def _(tile):
        cols = pl.ds(pl.multiple_of(tile * TILE, TILE), TILE)
        series = dot(map_ref[...], phases_ref[:, cols])
        series_ref[:, cols] = series
        offset = jnp.sum(series, axis=0, keepdims=True) / DATES
        rate = jnp.sum(epochs * series, axis=0, keepdims=True) / spread
        trend_ref[0, :, cols] = offset
        trend_ref[1, :, cols] = rate
        live = coherent_ref[:, cols].astype(F32)
        residual = (live * (series - offset - epochs * rate)).astype(BF16)
        spectrum_ref[...] += dot_nt(residual, table_ref[:, cols])

    def half_rows(half):
        return pl.ds(pl.multiple_of(half * HALF, HALF), HALF)

    def block(array, number):
        row, col = number // 4 * 32, number % 4 * 128
        return array[row : row + 32, col : col + 128]

    pl.semaphore_wait(barrier, 1 + PLANE - 1 + DEPTH - 1)

    theirs = spectrum_ref[half_rows(1 - section), :].astype(BF16)
    for number in range(PLANE):
        pair_out[number] = block(theirs, number)
    give = pltpu.make_async_remote_copy(
        src_ref=pair_out,
        dst_ref=pair_in,
        send_sem=send_sems.at[4],
        recv_sem=recv_sems.at[4],
        device_id=partner,
        device_id_type=MESH,
    )
    give.start()
    ours = spectrum_ref[half_rows(section), :]
    give.wait_recv()
    for number in range(PLANE):
        part_out[number] = (block(ours, number) + pair_in[number].astype(F32)).astype(BF16)

    def exchange(phase, mine, near, source, target):
        @pl.loop(1, PLANE)
        def _(hop):
            other, row, device = near(hop)
            pltpu.make_async_remote_copy(
                src_ref=source(other, row),
                dst_ref=target.at[mine],
                send_sem=send_sems.at[phase],
                recv_sem=recv_sems.at[phase],
                device_id=device,
                device_id_type=MESH,
            ).start()

        target[mine] = source(mine, lax.rem(mine, SHELF))[...]

    def arrived(phase, target, sems):
        blocks = target.at[pl.ds(0, target.shape[0] - 1)]
        pltpu.make_async_copy(blocks, blocks, sems.at[phase]).wait()

    exchange(0, me, in_plane, lambda other, row: part_out.at[other], part_in)
    smooth = smooth_ref[...]
    smooth_high = smooth.astype(BF16)
    smooth_low = (smooth - smooth_high.astype(F32)).astype(BF16)
    regroup, ungroup = regroup_matrix(False), regroup_matrix(True)
    arrived(0, part_in, recv_sems)
    row_sum = jnp.sum(part_in[...].astype(F32).reshape(2, 256, 128), axis=0).astype(BF16)
    up_out[...] = dot(regroup, row_sum).astype(BF16).reshape(DEPTH, 16, 128)
    exchange(1, z, along_z, lambda other, row: up_out.at[other], up_in)
    arrived(1, up_in, recv_sems)
    rows = up_in[...].reshape(256, 128)
    smoothed = dot(smooth_high, rows) + dot(smooth_low, rows)
    down_out[...] = (smoothed * scale_ref[me % 2]).astype(BF16).reshape(DEPTH, 16, 128)
    exchange(2, z, along_z, lambda other, row: down_out.at[other], down_in)
    arrived(2, down_in, recv_sems)
    whole = down_in[...].reshape(256, 128)
    back_out[...] = dot(ungroup, whole).astype(BF16).reshape(SHELF, 32, 128)
    exchange(3, me, in_plane, lambda other, row: back_out.at[row], back_in)
    arrived(3, back_in, recv_sems)

    swap = pltpu.make_async_remote_copy(
        src_ref=back_in,
        dst_ref=swap_in,
        send_sem=send_sems.at[5],
        recv_sem=recv_sems.at[5],
        device_id=partner,
        device_id_type=MESH,
    )
    swap.start()

    def correct(half, weights):
        for number in range(PLANE):
            row, col = number // 4 * 32, number % 4 * 128
            flat_ref[row : row + 32, col : col + 128] = weights[number]
        dates = half_rows(half)

        @pl.loop(0, COL_DEV // TILE)
        def _(tile):
            cols = pl.ds(pl.multiple_of(tile * TILE, TILE), TILE)
            screen = dot(flat_ref[...], table_ref[:, cols]).astype(BF16).astype(F32)
            live = coherent_ref[:, cols].astype(F32)
            corrected_ref[dates, cols] = (live * (series_ref[dates, cols] - screen)).astype(BF16)

    correct(section, back_in)
    give.wait_send()
    arrived(0, part_in, send_sems)
    arrived(1, up_in, send_sems)
    arrived(2, down_in, send_sems)
    arrived(3, back_in, send_sems)
    swap.wait_recv()
    correct(1 - section, swap_in)
    swap.wait_send()


def store_kernel(corrected_ref, trend_ref, corrected_hbm, trend_hbm, sems):
    stores = [
        pltpu.make_async_copy(corrected_ref, corrected_hbm, sems.at[0]),
        pltpu.make_async_copy(trend_ref, trend_hbm, sems.at[1]),
    ]
    for store in stores:
        store.start()
    for store in stores:
        store.wait()


def per_device(phases, incidence, coherent):
    ifgs = phases.shape[0]
    in_hbm = pl.BlockSpec(memory_space=pltpu.HBM)
    in_vmem = pl.BlockSpec(memory_space=pltpu.VMEM)
    results = (
        jax.ShapeDtypeStruct((DATES, COL_DEV), BF16),
        jax.ShapeDtypeStruct((2, 1, COL_DEV), F32),
    )
    operands = (
        incidence.T,
        coherent,
        jnp.asarray(angle_tables()),
        jnp.asarray(smoothing_matrix()),
        jnp.asarray(column_scales()),
        phases.reshape(ifgs, COL_DEV),
    )
    corrected, trend_fit = pl.pallas_call(
        screen_kernel,
        out_shape=results,
        in_specs=[in_hbm] * 6,
        out_specs=(in_vmem, in_vmem),
        scratch_shapes=[
            pltpu.VMEM((2, ifgs), jnp.int32),
            pltpu.VMEM((1, COL_DEV), jnp.int32),
            pltpu.VMEM((4, FREQS, 128), F32),
            pltpu.VMEM((256, 256), F32),
            pltpu.VMEM((2, 1, 128), F32),
            pltpu.VMEM((ifgs, COL_DEV), BF16),
            pltpu.VMEM((2 * FREQS, COL_DEV), BF16),
            pltpu.VMEM((DATES, COL_DEV), F32),
            pltpu.VMEM((DATES, 2 * FREQS), F32),
            pltpu.VMEM((DATES, ifgs), BF16),
            pltpu.VMEM((DATES, DATES), F32),
            pltpu.VMEM((PLANE, 32, 128), BF16),
            pltpu.VMEM((PLANE, 32, 128), BF16),
            pltpu.VMEM((PLANE, 32, 128), BF16),
            pltpu.VMEM((PLANE, 32, 128), BF16),
            pltpu.VMEM((DEPTH, 16, 128), BF16),
            pltpu.VMEM((DEPTH, 16, 128), BF16),
            pltpu.VMEM((DEPTH, 16, 128), BF16),
            pltpu.VMEM((DEPTH, 16, 128), BF16),
            pltpu.VMEM((SHELF, 32, 128), BF16),
            pltpu.VMEM((PLANE, 32, 128), BF16),
            pltpu.VMEM((PLANE, 32, 128), BF16),
            pltpu.VMEM((HALF, 2 * FREQS), BF16),
            pltpu.SemaphoreType.DMA((6,)),
            pltpu.SemaphoreType.DMA((6,)),
            pltpu.SemaphoreType.DMA((6,)),
        ],
        compiler_params=pltpu.CompilerParams(
            collective_id=0, has_side_effects=True, vmem_limit_bytes=36 * 2**20
        ),
        name="screen",
    )(*(pltpu.with_memory_space_constraint(operand, pltpu.HBM) for operand in operands))
    corrected, trend_fit = pl.pallas_call(
        store_kernel,
        out_shape=results,
        in_specs=[in_vmem] * 2,
        out_specs=(in_hbm, in_hbm),
        scratch_shapes=[pltpu.SemaphoreType.DMA((2,))],
        compiler_params=pltpu.CompilerParams(vmem_limit_bytes=8 * 2**20),
        name="store",
    )(corrected, trend_fit)
    return (corrected.reshape(DATES, 1, COL_DEV), trend_fit)


def solution(mesh):
    placed = (P(None, "grp", ("section", "sub")), P(), P("grp", ("section", "sub")))
    return jax.shard_map(
        per_device,
        mesh=mesh,
        in_specs=placed,
        out_specs=(P(None, "grp", ("section", "sub")), P(None, "grp", ("section", "sub"))),
        check_vma=False,
    )
```

```python
import functools
import math

import jax
import jax.numpy as jnp
import numpy as np
from jax import lax
from jax.experimental import pallas as pl
from jax.experimental.pallas import tpu as pltpu
from jax.sharding import PartitionSpec as P

MESH = pl.DeviceIdType.MESH
F32 = jnp.float32
BF16 = jnp.bfloat16

REG = 0.1
FREQS = 256
DATES = 256
ROWS = 128
COLS = 8192
BLOCKS = DATES // 8
COL_DEV = 2048
TILE = 512

PLANE = 16
HALF = DATES // 2
DEPTH = 16
SHELF = 8


def angle_tables():
    frequency = np.arange(FREQS, dtype=np.int64)[:, None]
    column = np.arange(128, dtype=np.int64)[None, :]
    start = (frequency * column % COLS) * (2.0 * math.pi / COLS)
    step = (frequency * np.full_like(column, 128) % COLS) * (2.0 * math.pi / COLS)
    return np.stack([np.cos(start), np.sin(start), np.cos(step), np.sin(step)]).astype(np.float32)


def row_filter():
    indices = np.arange(ROWS)
    frequency = np.minimum(indices, ROWS - indices).astype(np.float64)
    taper = np.exp(-np.square(frequency / (ROWS / 4.0)))
    turns = (indices[:, None] * indices[None, :] % ROWS) * (2.0 * math.pi / ROWS)
    cos_rows, sin_rows = np.cos(turns), np.sin(turns)
    return ((cos_rows * taper) @ cos_rows.T + (sin_rows * taper) @ sin_rows.T) / ROWS


def smoothing_matrix():
    index = np.arange(DEPTH * SHELF * 2)
    z, shelf, half = index // 16, index // 2 % 8, index % 2
    row = shelf // 4 * 64 + z * 4 + shelf % 4
    full = row_filter()[row[:, None], row[None, :]] * (half[:, None] == half[None, :])
    return full.astype(np.float32)


def column_scales():
    frequency = np.arange(FREQS)
    scale = np.where(frequency == 0, 1.0, 2.0) * np.exp(-np.square(frequency / FREQS)) / COLS
    return scale.astype(np.float32).reshape(2, 1, 128)


def iota(shape, axis):
    return lax.broadcasted_iota(jnp.int32, shape, axis)


def hot(condition):
    return jnp.where(condition, 1.0, 0.0).astype(F32)


def dot(a, b):
    return jnp.dot(a, b, preferred_element_type=F32)


def dot_nt(a, b):
    return lax.dot_general(a, b, (((1,), (1,)), ((), ())), preferred_element_type=F32)


def lane_roll(x, shift):
    flat = x.reshape(64, 128)
    return pltpu.roll(flat, shift, 1).reshape(8, 8, 128)


def block_product(a, b):
    terms = [a[:, k : k + 1, :] * b[k][None] for k in range(8)]
    while len(terms) > 1:
        terms = [one + two for one, two in zip(terms[::2], terms[1::2])]
    return terms[0]


def reciprocal(x):
    guess = pl.reciprocal(x, approx=True)
    guess = guess * (2.0 - x * guess)
    return guess * (2.0 - x * guess)


def block_inverse(d):
    sub = iota((8, 128), 0)
    rows = [d[i] for i in range(8)]
    for k in range(0, 8, 2):
        a, b = rows[k][k : k + 1, :], rows[k][k + 1 : k + 2, :]
        c, e = rows[k + 1][k : k + 1, :], rows[k + 1][k + 1 : k + 2, :]
        scale = reciprocal(a * e - b * c)
        one, two = sub == k, sub == k + 1
        first = jnp.where(one, 1.0, jnp.where(two, 0.0, rows[k]))
        second = jnp.where(one, 0.0, jnp.where(two, 1.0, rows[k + 1]))
        top = (e * scale) * first - (b * scale) * second
        bottom = (a * scale) * second - (c * scale) * first
        for i in range(8):
            if i not in (k, k + 1):
                f, g = rows[i][k : k + 1, :], rows[i][k + 1 : k + 2, :]
                rest = jnp.where(one | two, 0.0, rows[i])
                rows[i] = rest - (f * top + g * bottom)
        rows[k], rows[k + 1] = top, bottom
    return jnp.stack(rows)


def split(x):
    high = x.astype(BF16)
    return high, (x - high.astype(F32)).astype(BF16)


def dot_split(a, b):
    (ah, al), (bh, bl) = a, b
    return dot(jnp.concatenate([al, ah, ah], axis=1), jnp.concatenate([bh, bl, bh], axis=0))


def pseudo_inverse(incidence, beside):
    count = incidence.shape[1]
    primary, secondary = incidence[0:1, :], incidence[1:2, :]
    dates = iota((DATES, count), 0)
    design_t = hot(dates == secondary) - hot(dates == primary)
    p_in, p_block, s_in, s_block = primary & 7, primary >> 3, secondary & 7, secondary >> 3
    block = iota((128, count), 0) & (BLOCKS - 1)
    at_primary = hot(block == p_block).astype(BF16)
    at_secondary = hot(block == s_block).astype(BF16)
    pair = iota((64, count), 0)
    same = hot(p_block == s_block)
    ps = hot(pair == p_in * 8 + s_in)
    sp = hot(pair == s_in * 8 + p_in)
    on_primary = hot(pair == p_in * 9) - same * (ps + sp)
    on_secondary = hot(pair == s_in * 9)
    to_next = (same - 1.0) * ps
    to_last = (same - 1.0) * sp
    from_primary = dot_nt(jnp.concatenate([on_primary, to_next], 0).astype(BF16), at_primary)
    from_secondary = dot_nt(jnp.concatenate([on_secondary, to_last], 0).astype(BF16), at_secondary)
    entry = iota((64, 128), 0)
    eye = hot((entry >> 3) == (entry & 7))
    diag = (from_primary[:64] + from_secondary[:64] + REG * eye).reshape(8, 8, 128)
    below = from_secondary[64:].reshape(8, 8, 128)
    above = from_primary[64:].reshape(8, 8, 128)
    first = (iota((8, 8, 128), 2) & BLOCKS) == 0

    date = iota((2 * DATES, 128), 0)
    take = hot((date >> 3) == iota((2 * DATES, 128), 1)).astype(BF16)
    own_row = ((iota((2 * DATES, 128), 1) >> 3) & 7) == (iota((2 * DATES, 128), 0) & 7)
    spread = hot((iota((128, DATES), 1) & 7) == (iota((128, DATES), 0) & 7)).astype(BF16)
    row_block = iota((DATES, DATES), 0) >> 3
    col_block = iota((DATES, DATES), 1) >> 3

    def blocks_of(x, sides):
        count = sides * DATES
        terms = jnp.concatenate(split(x.reshape(64, 128)), axis=0)
        rows = jnp.where(own_row[:count], dot_nt(take[:count], terms), 0.0).astype(BF16)
        return dot(rows, spread)

    total = None
    step = 1
    while step < BLOCKS:
        beside()
        inverse = block_inverse(diag)
        near = jnp.where(first, lane_roll(inverse, step), lane_roll(inverse, 128 - step))
        gain = block_product(jnp.where(first, below, above), near)
        back = jnp.where(first, lane_roll(above, step), lane_roll(below, 128 - step))
        change = block_product(gain, back)
        diag = diag - change - lane_roll(change, BLOCKS)
        sides = blocks_of(gain, 2)
        gamma = jnp.where(
            col_block == row_block - step,
            sides[:DATES],
            jnp.where(col_block == row_block + step, sides[DATES:], 0.0),
        )
        if total is None:
            total = hot(iota((DATES, DATES), 0) == iota((DATES, DATES), 1)) - gamma
        else:
            total = total - dot_split(split(gamma), split(total))
        if 2 * step < BLOCKS:
            far = jnp.where(first, lane_roll(below, step), lane_roll(above, 128 - step))
            links = -block_product(gain, far)
            swapped = lane_roll(links, BLOCKS)
            below = jnp.where(first, links, swapped)
            above = jnp.where(first, swapped, links)
        step *= 2
    design_t = design_t.astype(BF16)
    reduced = dot(
        jnp.concatenate(split(total)[::-1], axis=1),
        jnp.concatenate([design_t, design_t], axis=0),
    )
    final = jnp.where(col_block == row_block, blocks_of(block_inverse(diag), 1), 0.0)
    return dot_split(split(final), split(reduced)).astype(BF16)


def part_index():
    return lax.axis_index("section") * 2 + lax.axis_index("sub")


def table_filler(angles_ref, table_ref):
    part = part_index()

    def fill(first):
        rows, sin_rows = slice(first, first + 64), slice(FREQS + first, FREQS + first + 64)
        cos, sin = angles_ref[0, rows, :], angles_ref[1, rows, :]
        step_cos, step_sin = angles_ref[2, rows, :], angles_ref[3, rows, :]
        quarter = ((iota((64, 128), 0) + first) * part) & 3
        odd, flip = (quarter & 1) == 1, quarter >= 2
        cos, sin = jnp.where(odd, -sin, cos), jnp.where(odd, cos, sin)
        cos, sin = jnp.where(flip, -cos, cos), jnp.where(flip, -sin, sin)
        cos_last, minus_last = cos * step_cos + sin * step_sin, cos * step_sin - sin * step_cos
        minus, twice = -sin, 2.0 * step_cos
        for tile in range(COL_DEV // 128):
            cols = slice(tile * 128, tile * 128 + 128)
            table_ref[rows, cols] = cos.astype(BF16)
            table_ref[sin_rows, cols] = minus.astype(BF16)
            cos, cos_last = twice * cos - cos_last, cos
            minus, minus_last = twice * minus - minus_last, minus

    steps = [functools.partial(fill, first) for first in range(0, FREQS, 64)]
    return lambda: steps.pop()() if steps else None


def regroup_matrix(inverse):
    out, source = iota((256, 256), 0), iota((256, 256), 1)
    if inverse:
        out, source = source, out
    return hot(source == ((out >> 1) & 7) * 32 + (out >> 4) * 2 + (out & 1)).astype(BF16)


def screen_kernel(
    incidence_hbm,
    coherent_hbm,
    angles_hbm,
    smooth_hbm,
    scale_hbm,
    phases_hbm,
    corrected_ref,
    trend_ref,
    incidence_ref,
    coherent_ref,
    angles_ref,
    smooth_ref,
    scale_ref,
    phases_ref,
    table_ref,
    series_ref,
    residual_ref,
    map_ref,
    pair_out,
    pair_in,
    part_out,
    part_in,
    up_out,
    up_in,
    down_out,
    down_in,
    back_out,
    back_in,
    swap_in,
    flat_ref,
    load_sems,
    send_sems,
    recv_sems,
):
    loads = [
        pltpu.make_async_copy(source, target, load_sems.at[i])
        for i, (source, target) in enumerate(
            [
                (incidence_hbm, incidence_ref),
                (angles_hbm, angles_ref),
                (coherent_hbm, coherent_ref),
                (phases_hbm, phases_ref),
                (smooth_hbm, smooth_ref),
                (scale_hbm, scale_ref),
            ]
        )
    ]
    for load in loads:
        load.start()

    section, grp, sub = (lax.axis_index(name) for name in ("section", "grp", "sub"))
    y, z, x = grp // 64, grp // 4 % 16, grp % 4
    me = sub * 8 + y * 4 + x
    subs, ys = (sub, 1 - sub), (y, 1 - y)
    xs = [(x + hop) % 4 for hop in (2, 1, 3, 0)]
    zs = [(z + hop) % 16 for hop in (8, 7, 9, 6, 10, 5, 11, 4, 12, 3, 13, 2, 14, 1, 15)]
    plane = [
        (b * 8 + c * 4 + d, c * 4 + d, (section, c * 64 + z * 4 + d, b))
        for d in xs
        for b in subs[::-1]
        for c in ys[::-1]
    ][:-1]
    column = [(other, other, (section, y * 64 + other * 4 + x, sub)) for other in zs]
    partner = (1 - section, grp, sub)

    barrier = pltpu.get_barrier_semaphore()
    for device in [partner] + [device for _, _, device in plane + column]:
        pl.semaphore_signal(barrier, inc=1, device_id=device, device_id_type=MESH)

    loads[0].wait()
    loads[1].wait()
    map_ref[...] = pseudo_inverse(incidence_ref[...], table_filler(angles_ref, table_ref))
    epochs = (2.0 * iota((DATES, 1), 0).astype(F32) - (DATES - 1)) / (DATES - 1)
    spread = sum(((2.0 * n - (DATES - 1)) / (DATES - 1)) ** 2 for n in range(DATES))
    for load in loads[2:]:
        load.wait()

    for tile in range(COL_DEV // TILE):
        cols = slice(tile * TILE, tile * TILE + TILE)
        series = dot(map_ref[...], phases_ref[:, cols])
        series_ref[:, cols] = series
        offset = jnp.sum(series, axis=0, keepdims=True) / DATES
        rate = jnp.sum(epochs * series, axis=0, keepdims=True) / spread
        trend_ref[0, :, cols] = offset
        trend_ref[1, :, cols] = rate
        live = coherent_ref[:, cols].astype(F32)
        residual_ref[:, cols] = (live * (series - offset - epochs * rate)).astype(BF16)

    def half_rows(half):
        return pl.ds(pl.multiple_of(half * HALF, HALF), HALF)

    def block(array, number):
        row, col = number // 4 * 32, number % 4 * 128
        return array[row : row + 32, col : col + 128]

    pl.semaphore_wait(barrier, 1 + len(plane) + len(column))

    theirs = dot_nt(residual_ref[half_rows(1 - section), :], table_ref[...]).astype(BF16)
    for number in range(PLANE):
        pair_out[number] = block(theirs, number)
    give = pltpu.make_async_remote_copy(
        src_ref=pair_out,
        dst_ref=pair_in,
        send_sem=send_sems.at[4],
        recv_sem=recv_sems.at[4],
        device_id=partner,
        device_id_type=MESH,
    )
    give.start()
    ours = dot_nt(residual_ref[half_rows(section), :], table_ref[...])
    give.wait_recv()
    for number in range(PLANE):
        part_out[number] = (block(ours, number) + pair_in[number].astype(F32)).astype(BF16)

    def exchange(phase, mine, partners, source, target):
        for other, row, device in partners:
            pltpu.make_async_remote_copy(
                src_ref=source(other, row),
                dst_ref=target.at[mine],
                send_sem=send_sems.at[phase],
                recv_sem=recv_sems.at[phase],
                device_id=device,
                device_id_type=MESH,
            ).start()
        target[mine] = source(mine, lax.rem(mine, SHELF))[...]

    def arrived(phase, target, sems):
        blocks = target.at[pl.ds(0, target.shape[0] - 1)]
        pltpu.make_async_copy(blocks, blocks, sems.at[phase]).wait()

    exchange(0, me, plane, lambda other, row: part_out.at[other], part_in)
    smooth = smooth_ref[...]
    smooth_high = smooth.astype(BF16)
    smooth_low = (smooth - smooth_high.astype(F32)).astype(BF16)
    regroup, ungroup = regroup_matrix(False), regroup_matrix(True)
    arrived(0, part_in, recv_sems)
    row_sum = jnp.sum(part_in[...].astype(F32).reshape(2, 256, 128), axis=0).astype(BF16)
    up_out[...] = dot(regroup, row_sum).astype(BF16).reshape(DEPTH, 16, 128)
    exchange(1, z, column, lambda other, row: up_out.at[other], up_in)
    arrived(1, up_in, recv_sems)
    rows = up_in[...].reshape(256, 128)
    smoothed = dot(smooth_high, rows) + dot(smooth_low, rows)
    down_out[...] = (smoothed * scale_ref[me % 2]).astype(BF16).reshape(DEPTH, 16, 128)
    exchange(2, z, column, lambda other, row: down_out.at[other], down_in)
    arrived(2, down_in, recv_sems)
    whole = down_in[...].reshape(256, 128)
    back_out[...] = dot(ungroup, whole).astype(BF16).reshape(SHELF, 32, 128)
    exchange(3, me, plane, lambda other, row: back_out.at[row], back_in)
    arrived(3, back_in, recv_sems)

    swap = pltpu.make_async_remote_copy(
        src_ref=back_in,
        dst_ref=swap_in,
        send_sem=send_sems.at[5],
        recv_sem=recv_sems.at[5],
        device_id=partner,
        device_id_type=MESH,
    )
    swap.start()

    def correct(half, weights):
        for number in range(PLANE):
            row, col = number // 4 * 32, number % 4 * 128
            flat_ref[row : row + 32, col : col + 128] = weights[number]
        dates = half_rows(half)
        for tile in range(COL_DEV // TILE):
            cols = slice(tile * TILE, tile * TILE + TILE)
            screen = dot(flat_ref[...], table_ref[:, cols]).astype(BF16).astype(F32)
            live = coherent_ref[:, cols].astype(F32)
            corrected_ref[dates, cols] = (live * (series_ref[dates, cols] - screen)).astype(BF16)

    correct(section, back_in)
    give.wait_send()
    arrived(0, part_in, send_sems)
    arrived(1, up_in, send_sems)
    arrived(2, down_in, send_sems)
    arrived(3, back_in, send_sems)
    swap.wait_recv()
    correct(1 - section, swap_in)
    swap.wait_send()


def store_kernel(corrected_ref, trend_ref, corrected_hbm, trend_hbm, sems):
    stores = [
        pltpu.make_async_copy(corrected_ref, corrected_hbm, sems.at[0]),
        pltpu.make_async_copy(trend_ref, trend_hbm, sems.at[1]),
    ]
    for store in stores:
        store.start()
    for store in stores:
        store.wait()


def per_device(phases, incidence, coherent):
    ifgs = phases.shape[0]
    in_hbm = pl.BlockSpec(memory_space=pltpu.HBM)
    in_vmem = pl.BlockSpec(memory_space=pltpu.VMEM)
    results = (
        jax.ShapeDtypeStruct((DATES, COL_DEV), BF16),
        jax.ShapeDtypeStruct((2, 1, COL_DEV), F32),
    )
    operands = (
        incidence.T,
        coherent,
        jnp.asarray(angle_tables()),
        jnp.asarray(smoothing_matrix()),
        jnp.asarray(column_scales()),
        phases.reshape(ifgs, COL_DEV),
    )
    corrected, trend_fit = pl.pallas_call(
        screen_kernel,
        out_shape=results,
        in_specs=[in_hbm] * 6,
        out_specs=(in_vmem, in_vmem),
        scratch_shapes=[
            pltpu.VMEM((2, ifgs), jnp.int32),
            pltpu.VMEM((1, COL_DEV), jnp.int32),
            pltpu.VMEM((4, FREQS, 128), F32),
            pltpu.VMEM((256, 256), F32),
            pltpu.VMEM((2, 1, 128), F32),
            pltpu.VMEM((ifgs, COL_DEV), BF16),
            pltpu.VMEM((2 * FREQS, COL_DEV), BF16),
            pltpu.VMEM((DATES, COL_DEV), F32),
            pltpu.VMEM((DATES, COL_DEV), BF16),
            pltpu.VMEM((DATES, ifgs), BF16),
            pltpu.VMEM((PLANE, 32, 128), BF16),
            pltpu.VMEM((PLANE, 32, 128), BF16),
            pltpu.VMEM((PLANE, 32, 128), BF16),
            pltpu.VMEM((PLANE, 32, 128), BF16),
            pltpu.VMEM((DEPTH, 16, 128), BF16),
            pltpu.VMEM((DEPTH, 16, 128), BF16),
            pltpu.VMEM((DEPTH, 16, 128), BF16),
            pltpu.VMEM((DEPTH, 16, 128), BF16),
            pltpu.VMEM((SHELF, 32, 128), BF16),
            pltpu.VMEM((PLANE, 32, 128), BF16),
            pltpu.VMEM((PLANE, 32, 128), BF16),
            pltpu.VMEM((HALF, 2 * FREQS), BF16),
            pltpu.SemaphoreType.DMA((6,)),
            pltpu.SemaphoreType.DMA((6,)),
            pltpu.SemaphoreType.DMA((6,)),
        ],
        compiler_params=pltpu.CompilerParams(
            collective_id=0, has_side_effects=True, vmem_limit_bytes=36 * 2**20
        ),
        name="screen",
    )(*(pltpu.with_memory_space_constraint(operand, pltpu.HBM) for operand in operands))
    corrected, trend_fit = pl.pallas_call(
        store_kernel,
        out_shape=results,
        in_specs=[in_vmem] * 2,
        out_specs=(in_hbm, in_hbm),
        scratch_shapes=[pltpu.SemaphoreType.DMA((2,))],
        compiler_params=pltpu.CompilerParams(vmem_limit_bytes=8 * 2**20),
        name="store",
    )(corrected, trend_fit)
    return (corrected.reshape(DATES, 1, COL_DEV), trend_fit)


def solution(mesh):
    placed = (P(None, "grp", ("section", "sub")), P(), P("grp", ("section", "sub")))
    return jax.shard_map(
        per_device,
        mesh=mesh,
        in_specs=placed,
        out_specs=(P(None, "grp", ("section", "sub")), P(None, "grp", ("section", "sub"))),
        check_vma=False,
    )
```

```python
import math

import jax
import jax.numpy as jnp
import numpy as np
from jax import lax
from jax.experimental import pallas as pl
from jax.experimental.pallas import tpu as pltpu
from jax.sharding import PartitionSpec as P

MESH = pl.DeviceIdType.MESH
F32 = jnp.float32
BF16 = jnp.bfloat16

REG = 0.1
FREQS = 256
DATES = 256
ROWS = 128
COLS = 8192
BLOCKS = DATES // 8
COL_DEV = 2048
TILE = 512

PLANE = 16
HALF = DATES // 2
DEPTH = 16
SHELF = 8


def angle_tables():
    frequency = np.arange(FREQS, dtype=np.int64)[:, None]
    column = np.arange(128, dtype=np.int64)[None, :]
    start = (frequency * column % COLS) * (2.0 * math.pi / COLS)
    step = (frequency * np.full_like(column, 128) % COLS) * (2.0 * math.pi / COLS)
    return np.stack([np.cos(start), np.sin(start), np.cos(step), np.sin(step)]).astype(np.float32)


def row_filter():
    indices = np.arange(ROWS)
    frequency = np.minimum(indices, ROWS - indices).astype(np.float64)
    taper = np.exp(-np.square(frequency / (ROWS / 4.0)))
    turns = (indices[:, None] * indices[None, :] % ROWS) * (2.0 * math.pi / ROWS)
    cos_rows, sin_rows = np.cos(turns), np.sin(turns)
    return ((cos_rows * taper) @ cos_rows.T + (sin_rows * taper) @ sin_rows.T) / ROWS


def smoothing_matrix():
    index = np.arange(DEPTH * SHELF)
    z, shelf = index // 8, index % 8
    row = shelf // 4 * 64 + z * 4 + shelf % 4
    return row_filter()[row[:, None], row[None, :]].astype(np.float32)


def column_scales():
    frequency = np.arange(FREQS)
    scale = np.where(frequency == 0, 1.0, 2.0) * np.exp(-np.square(frequency / FREQS)) / COLS
    return np.repeat(scale.astype(np.float32)[:, None, None], 128, axis=2)


def iota(shape, axis):
    return lax.broadcasted_iota(jnp.int32, shape, axis)


def hot(condition):
    return jnp.where(condition, 1.0, 0.0).astype(F32)


def dot(a, b):
    return jnp.dot(a, b, preferred_element_type=F32)


def dot_nt(a, b):
    return lax.dot_general(a, b, (((1,), (1,)), ((), ())), preferred_element_type=F32)


def lane_roll(x, shift):
    flat = x.reshape(64, 128)
    return pltpu.roll(flat, shift, 1).reshape(8, 8, 128)


def block_product(a, b):
    terms = [a[:, k : k + 1, :] * b[k][None] for k in range(8)]
    while len(terms) > 1:
        terms = [one + two for one, two in zip(terms[::2], terms[1::2])]
    return terms[0]


def reciprocal(x):
    guess = pl.reciprocal(x, approx=True)
    guess = guess * (2.0 - x * guess)
    return guess * (2.0 - x * guess)


def block_inverse(d):
    sub = iota((8, 128), 0)
    rows = [d[i] for i in range(8)]
    for k in range(0, 8, 2):
        a, b = rows[k][k : k + 1, :], rows[k][k + 1 : k + 2, :]
        c, e = rows[k + 1][k : k + 1, :], rows[k + 1][k + 1 : k + 2, :]
        scale = reciprocal(a * e - b * c)
        one, two = sub == k, sub == k + 1
        first = jnp.where(one, 1.0, jnp.where(two, 0.0, rows[k]))
        second = jnp.where(one, 0.0, jnp.where(two, 1.0, rows[k + 1]))
        top = (e * scale) * first - (b * scale) * second
        bottom = (a * scale) * second - (c * scale) * first
        for i in range(8):
            if i not in (k, k + 1):
                f, g = rows[i][k : k + 1, :], rows[i][k + 1 : k + 2, :]
                rest = jnp.where(one | two, 0.0, rows[i])
                rows[i] = rest - (f * top + g * bottom)
        rows[k], rows[k + 1] = top, bottom
    return jnp.stack(rows)


def split(x):
    high = x.astype(BF16)
    return high, (x - high.astype(F32)).astype(BF16)


def dot_split(a, b):
    (ah, al), (bh, bl) = a, b
    return dot(jnp.concatenate([al, ah, ah], axis=1), jnp.concatenate([bh, bl, bh], axis=0))


def split_fully(x):
    high, _ = split(x)
    return (high, *split(x - high.astype(F32)))


def dot_nt_fully(a, b):
    (ah, am, al), (bh, bm, bl) = split_fully(a), split_fully(b)
    return dot_nt(
        jnp.concatenate([al, am, ah, am, ah, ah], axis=1),
        jnp.concatenate([bh, bm, bl, bh, bm, bh], axis=1),
    )


def design_rows(incidence):
    dates = iota((DATES, incidence.shape[1]), 0)
    return (hot(dates == incidence[1:2, :]) - hot(dates == incidence[0:1, :])).astype(BF16)


def pseudo_inverse(incidence, design_t):
    count = incidence.shape[1]
    primary, secondary = incidence[0:1, :], incidence[1:2, :]
    p_in, p_block, s_in, s_block = primary & 7, primary >> 3, secondary & 7, secondary >> 3
    block = iota((128, count), 0) & (BLOCKS - 1)
    at_primary = hot(block == p_block).astype(BF16)
    at_secondary = hot(block == s_block).astype(BF16)
    pair = iota((64, count), 0)
    same = hot(p_block == s_block)
    ps = hot(pair == p_in * 8 + s_in)
    sp = hot(pair == s_in * 8 + p_in)
    on_primary = hot(pair == p_in * 9) - same * (ps + sp)
    on_secondary = hot(pair == s_in * 9)
    to_next = (same - 1.0) * ps
    to_last = (same - 1.0) * sp
    from_primary = dot_nt(jnp.concatenate([on_primary, to_next], 0).astype(BF16), at_primary)
    from_secondary = dot_nt(jnp.concatenate([on_secondary, to_last], 0).astype(BF16), at_secondary)
    entry = iota((64, 128), 0)
    eye = hot((entry >> 3) == (entry & 7))
    diag = (from_primary[:64] + from_secondary[:64] + REG * eye).reshape(8, 8, 128)
    below = from_secondary[64:].reshape(8, 8, 128)
    above = from_primary[64:].reshape(8, 8, 128)
    first = (iota((8, 8, 128), 2) & BLOCKS) == 0

    date = iota((2 * DATES, 128), 0)
    take = hot((date >> 3) == iota((2 * DATES, 128), 1)).astype(BF16)
    own_row = ((iota((2 * DATES, 128), 1) >> 3) & 7) == (iota((2 * DATES, 128), 0) & 7)
    spread = hot((iota((128, DATES), 1) & 7) == (iota((128, DATES), 0) & 7)).astype(BF16)
    row_block = iota((DATES, DATES), 0) >> 3
    col_block = iota((DATES, DATES), 1) >> 3

    def blocks_of(x, sides):
        count = sides * DATES
        terms = jnp.concatenate(split(x.reshape(64, 128)), axis=0)
        rows = jnp.where(own_row[:count], dot_nt(take[:count], terms), 0.0).astype(BF16)
        return dot(rows, spread)

    total = None
    step = 1
    while step < BLOCKS:
        inverse = block_inverse(diag)
        near = jnp.where(first, lane_roll(inverse, step), lane_roll(inverse, 128 - step))
        gain = block_product(jnp.where(first, below, above), near)
        back = jnp.where(first, lane_roll(above, step), lane_roll(below, 128 - step))
        change = block_product(gain, back)
        diag = diag - change - lane_roll(change, BLOCKS)
        sides = blocks_of(gain, 2)
        gamma = jnp.where(
            col_block == row_block - step,
            sides[:DATES],
            jnp.where(col_block == row_block + step, sides[DATES:], 0.0),
        )
        if total is None:
            total = hot(iota((DATES, DATES), 0) == iota((DATES, DATES), 1)) - gamma
        else:
            total = total - dot_split(split(gamma), split(total))
        if 2 * step < BLOCKS:
            far = jnp.where(first, lane_roll(below, step), lane_roll(above, 128 - step))
            links = -block_product(gain, far)
            swapped = lane_roll(links, BLOCKS)
            below = jnp.where(first, links, swapped)
            above = jnp.where(first, swapped, links)
        step *= 2
        yield
    reduced = dot(
        jnp.concatenate(split(total)[::-1], axis=1),
        jnp.concatenate([design_t, design_t], axis=0),
    )
    final = jnp.where(col_block == row_block, blocks_of(block_inverse(diag), 1), 0.0)
    yield dot_split(split(final), split(reduced)).astype(BF16), total, final


def part_index():
    return lax.axis_index("section") * 2 + lax.axis_index("sub")


def fill_table(angles_ref, table_ref):
    part = part_index()

    def fill(first):
        rows, sin_rows = slice(first, first + 64), slice(FREQS + first, FREQS + first + 64)
        cos, sin = angles_ref[0, rows, :], angles_ref[1, rows, :]
        step_cos, step_sin = angles_ref[2, rows, :], angles_ref[3, rows, :]
        quarter = ((iota((64, 128), 0) + first) * part) & 3
        odd, flip = (quarter & 1) == 1, quarter >= 2
        cos, sin = jnp.where(odd, -sin, cos), jnp.where(odd, cos, sin)
        cos, sin = jnp.where(flip, -cos, cos), jnp.where(flip, -sin, sin)
        cos_last, minus_last = cos * step_cos + sin * step_sin, cos * step_sin - sin * step_cos
        minus, twice = -sin, 2.0 * step_cos
        for tile in range(COL_DEV // 128):
            cols = slice(tile * 128, tile * 128 + 128)
            table_ref[rows, cols] = cos.astype(BF16)
            table_ref[sin_rows, cols] = minus.astype(BF16)
            cos, cos_last = twice * cos - cos_last, cos
            minus, minus_last = twice * minus - minus_last, minus

    for first in range(0, FREQS, 64):
        fill(first)


def regroup_matrix():
    out, source = iota((128, 128), 0), iota((128, 128), 1)
    return hot(source == (out & 7) * 16 + (out >> 3)).astype(BF16)


def ungroup_matrix():
    out, source = iota((256, 256), 0), iota((256, 256), 1)
    return hot(source == (out & 15) * 16 + ((out >> 4) & 1) * 8 + (out >> 5)).astype(BF16)


def screen_kernel(
    incidence_hbm,
    coherent_hbm,
    angles_hbm,
    smooth_hbm,
    scale_hbm,
    phases_hbm,
    corrected_ref,
    trend_ref,
    incidence_ref,
    coherent_ref,
    angles_ref,
    smooth_ref,
    scale_ref,
    phases_ref,
    table_ref,
    series_ref,
    live_ref,
    map_ref,
    pair_out,
    pair_in,
    part_out,
    part_in,
    up_out,
    up_in,
    down_out,
    down_in,
    back_out,
    back_in,
    swap_in,
    flat_ref,
    load_sems,
    send_sems,
    recv_sems,
):
    loads = [
        pltpu.make_async_copy(source, target, load_sems.at[i])
        for i, (source, target) in enumerate(
            [
                (incidence_hbm, incidence_ref),
                (angles_hbm, angles_ref),
                (coherent_hbm, coherent_ref),
                (phases_hbm, phases_ref),
                (smooth_hbm, smooth_ref),
                (scale_hbm, scale_ref),
            ]
        )
    ]
    for load in loads:
        load.start()

    section, grp, sub = (lax.axis_index(name) for name in ("section", "grp", "sub"))
    y, z, x = grp // 64, grp // 4 % 16, grp % 4
    me = sub * 8 + y * 4 + x
    subs, ys = (sub, 1 - sub), (y, 1 - y)
    xs = [(x + hop) % 4 for hop in (2, 1, 3, 0)]
    zs = [(z + hop) % 16 for hop in (8, 7, 9, 6, 10, 5, 11, 4, 12, 3, 13, 2, 14, 1, 15)]
    plane = [
        (b * 8 + c * 4 + d, c * 4 + d, (section, c * 64 + z * 4 + d, b))
        for d in xs
        for b in subs[::-1]
        for c in ys[::-1]
    ][:-1]
    column = [(other, other, (section, y * 64 + other * 4 + x, sub)) for other in zs]
    partner = (1 - section, grp, sub)

    barrier = pltpu.get_barrier_semaphore()
    for device in [partner] + [device for _, _, device in plane + column]:
        pl.semaphore_signal(barrier, inc=1, device_id=device, device_id_type=MESH)

    loads[1].wait()
    fill_table(angles_ref, table_ref)
    loads[0].wait()
    design_t = design_rows(incidence_ref[...])
    for load in loads[2:]:
        load.wait()

    for tile in range(COL_DEV // TILE):
        cols = slice(tile * TILE, tile * TILE + TILE)
        live = coherent_ref[:, cols].astype(F32)
        live_ref[0, :, cols], live_ref[1, :, cols] = split(live * dot(design_t, phases_ref[:, cols]))

    def spectrum(half):
        table = table_ref[pl.ds(pl.multiple_of(half * FREQS, FREQS), FREQS), :]
        return dot_nt(table, live_ref[1]) + dot_nt(table, live_ref[0])

    pl.semaphore_wait(barrier, 1 + len(plane) + len(column))

    pair_out[...] = spectrum(1 - section)
    give = pltpu.make_async_remote_copy(
        src_ref=pair_out,
        dst_ref=pair_in,
        send_sem=send_sems.at[4],
        recv_sem=recv_sems.at[4],
        device_id=partner,
        device_id_type=MESH,
    )
    give.start()
    ours = spectrum(section)
    give.wait_recv()
    part_out[...] = (ours + pair_in[...]).reshape(PLANE, 16, DATES)

    def exchange(phase, mine, partners, source, target):
        for other, row, device in partners:
            pltpu.make_async_remote_copy(
                src_ref=source(other, row),
                dst_ref=target.at[mine],
                send_sem=send_sems.at[phase],
                recv_sem=recv_sems.at[phase],
                device_id=device,
                device_id_type=MESH,
            ).start()
        target[mine] = source(mine, lax.rem(mine, SHELF))[...]

    def arrived(phase, target, sems):
        blocks = target.at[pl.ds(0, target.shape[0] - 1)]
        pltpu.make_async_copy(blocks, blocks, sems.at[phase]).wait()

    exchange(0, me, plane, lambda other, row: part_out.at[other], part_in)
    inverting = pseudo_inverse(incidence_ref[...], design_t)
    regroup = regroup_matrix()
    next(inverting)
    next(inverting)
    arrived(0, part_in, recv_sems)
    row_sum = jnp.sum(part_in[...].reshape(2, 128, DATES), axis=0)
    terms = jnp.concatenate(split_fully(row_sum), axis=0)
    rows = dot(jnp.concatenate([regroup, regroup, regroup], axis=1), terms)
    up_out[...] = rows.reshape(DEPTH, SHELF, DATES)
    exchange(1, z, column, lambda other, row: up_out.at[other], up_in)
    steps = list(inverting)
    map_ref[...], total, final = steps[-1]
    epochs = (2.0 * iota((DATES, 1), 0).astype(F32) - (DATES - 1)) / (DATES - 1)
    epochs_row = (2.0 * iota((1, DATES), 1).astype(F32) - (DATES - 1)) / (DATES - 1)
    spread = sum(((2.0 * n - (DATES - 1)) / (DATES - 1)) ** 2 for n in range(DATES))
    arrived(1, up_in, recv_sems)
    rows = dot_nt_fully(dot_nt_fully(up_in[...].reshape(128, DATES), total), final)
    offset = jnp.sum(rows, axis=1, keepdims=True) / DATES
    rate = jnp.sum(rows * epochs_row, axis=1, keepdims=True) / spread
    rows = rows - offset - rate * epochs_row
    smoothed = dot_split(split(smooth_ref[...]), split(rows))
    scale = scale_ref[me * 16 + z]
    halves = [
        (smoothed[:, first : first + 128] * scale).reshape(DEPTH, SHELF, 128)
        for first in (0, 128)
    ]
    down_out[...] = jnp.concatenate(halves, axis=1).astype(BF16)
    exchange(2, z, column, lambda other, row: down_out.at[other], down_in)

    for tile in range(COL_DEV // TILE):
        cols = slice(tile * TILE, tile * TILE + TILE)
        series = dot(map_ref[...], phases_ref[:, cols])
        series_ref[:, cols] = series
        trend_ref[0, :, cols] = jnp.sum(series, axis=0, keepdims=True) / DATES
        trend_ref[1, :, cols] = jnp.sum(epochs * series, axis=0, keepdims=True) / spread

    ungroup = ungroup_matrix()
    arrived(2, down_in, recv_sems)
    whole = down_in[...].reshape(256, 128)
    back_out[...] = dot(ungroup, whole).astype(BF16).reshape(SHELF, 32, 128)
    exchange(3, me, plane, lambda other, row: back_out.at[row], back_in)
    arrived(3, back_in, recv_sems)

    swap = pltpu.make_async_remote_copy(
        src_ref=back_in,
        dst_ref=swap_in,
        send_sem=send_sems.at[5],
        recv_sem=recv_sems.at[5],
        device_id=partner,
        device_id_type=MESH,
    )
    swap.start()

    def keep(half, weights):
        for number in range(PLANE):
            first = pl.multiple_of(half * FREQS + number * 16, 16)
            for dates in (0, 1):
                flat_ref[pl.ds(first, 16), dates * 128 : dates * 128 + 128] = weights[
                    number, dates * 16 : dates * 16 + 16
                ]

    keep(section, back_in)
    give.wait_send()
    arrived(0, part_in, send_sems)
    arrived(1, up_in, send_sems)
    arrived(2, down_in, send_sems)
    arrived(3, back_in, send_sems)
    swap.wait_recv()
    keep(1 - section, swap_in)
    eye = hot(iota((DATES, DATES), 0) == iota((DATES, DATES), 1)).astype(BF16)
    weights = dot_nt(eye, flat_ref[...]).astype(BF16)
    for tile in range(COL_DEV // TILE):
        cols = slice(tile * TILE, tile * TILE + TILE)
        screen = dot(weights, table_ref[:, cols]).astype(BF16).astype(F32)
        live = coherent_ref[:, cols].astype(F32)
        corrected_ref[:, cols] = (live * (series_ref[:, cols] - screen)).astype(BF16)
    swap.wait_send()


def store_kernel(corrected_ref, trend_ref, corrected_hbm, trend_hbm, sems):
    stores = [
        pltpu.make_async_copy(corrected_ref, corrected_hbm, sems.at[0]),
        pltpu.make_async_copy(trend_ref, trend_hbm, sems.at[1]),
    ]
    for store in stores:
        store.start()
    for store in stores:
        store.wait()


def per_device(phases, incidence, coherent):
    ifgs = phases.shape[0]
    in_hbm = pl.BlockSpec(memory_space=pltpu.HBM)
    in_vmem = pl.BlockSpec(memory_space=pltpu.VMEM)
    results = (
        jax.ShapeDtypeStruct((DATES, COL_DEV), BF16),
        jax.ShapeDtypeStruct((2, 1, COL_DEV), F32),
    )
    operands = (
        incidence.T,
        coherent,
        jnp.asarray(angle_tables()),
        jnp.asarray(smoothing_matrix()),
        jnp.asarray(column_scales()),
        phases.reshape(ifgs, COL_DEV),
    )
    corrected, trend_fit = pl.pallas_call(
        screen_kernel,
        out_shape=results,
        in_specs=[in_hbm] * 6,
        out_specs=(in_vmem, in_vmem),
        scratch_shapes=[
            pltpu.VMEM((2, ifgs), jnp.int32),
            pltpu.VMEM((1, COL_DEV), jnp.int32),
            pltpu.VMEM((4, FREQS, 128), F32),
            pltpu.VMEM((128, 128), F32),
            pltpu.VMEM((FREQS, 1, 128), F32),
            pltpu.VMEM((ifgs, COL_DEV), BF16),
            pltpu.VMEM((2 * FREQS, COL_DEV), BF16),
            pltpu.VMEM((DATES, COL_DEV), F32),
            pltpu.VMEM((2, DATES, COL_DEV), BF16),
            pltpu.VMEM((DATES, ifgs), BF16),
            pltpu.VMEM((FREQS, DATES), F32),
            pltpu.VMEM((FREQS, DATES), F32),
            pltpu.VMEM((PLANE, 16, DATES), F32),
            pltpu.VMEM((PLANE, 16, DATES), F32),
            pltpu.VMEM((DEPTH, SHELF, DATES), F32),
            pltpu.VMEM((DEPTH, SHELF, DATES), F32),
            pltpu.VMEM((DEPTH, 16, 128), BF16),
            pltpu.VMEM((DEPTH, 16, 128), BF16),
            pltpu.VMEM((SHELF, 32, 128), BF16),
            pltpu.VMEM((PLANE, 32, 128), BF16),
            pltpu.VMEM((PLANE, 32, 128), BF16),
            pltpu.VMEM((2 * FREQS, DATES), BF16),
            pltpu.SemaphoreType.DMA((6,)),
            pltpu.SemaphoreType.DMA((6,)),
            pltpu.SemaphoreType.DMA((6,)),
        ],
        compiler_params=pltpu.CompilerParams(
            collective_id=0, has_side_effects=True, vmem_limit_bytes=36 * 2**20
        ),
        name="screen",
    )(*(pltpu.with_memory_space_constraint(operand, pltpu.HBM) for operand in operands))
    corrected, trend_fit = pl.pallas_call(
        store_kernel,
        out_shape=results,
        in_specs=[in_vmem] * 2,
        out_specs=(in_hbm, in_hbm),
        scratch_shapes=[pltpu.SemaphoreType.DMA((2,))],
        compiler_params=pltpu.CompilerParams(vmem_limit_bytes=8 * 2**20),
        name="store",
    )(corrected, trend_fit)
    return (corrected.reshape(DATES, 1, COL_DEV), trend_fit)


def solution(mesh):
    placed = (P(None, "grp", ("section", "sub")), P(), P("grp", ("section", "sub")))
    return jax.shard_map(
        per_device,
        mesh=mesh,
        in_specs=placed,
        out_specs=(P(None, "grp", ("section", "sub")), P(None, "grp", ("section", "sub"))),
        check_vma=False,
    )
```
